128 devices in a mesh: subtree: 32 (over y, z, core), chan: 2 (over x_lo), fshard: 2 (over x_hi).
Axes of the slice: x: 4 (x_hi: 2, x_lo: 2; x = x_hi * 2 + x_lo), y: 4, z: 4, core: 2. Of those that a mesh axis runs over, the one named last changes fastest.
Arguments:
- leaf_rhs: float32 [131072, 256], P(('subtree', 'fshard'), 'chan'), may hold values from -6 to 6
- node_rhs: float32 [32768, 256], P(('subtree', 'fshard'), 'chan'), may hold values from -6 to 6
- leaf_inv: float32 [131072, 4096], P(('subtree', 'fshard')), as said below
- node_inv: float32 [32768, 1024], P(('subtree', 'fshard')), as said below
- leaf_panel: float32 [16384, 4096], P('subtree', 'fshard'), may hold values from -0.046875 to 0.046875
- node_panel: float32 [16384, 1024], P('subtree', 'fshard'), may hold values from -0.09375 to 0.09375
- leaf_rows: int32 [32, 512], P('subtree'), may hold values from 0 to 1023, as said below
- node_rows: int32 [32, 512], P('subtree'), may hold values from 0 to 1023, as said below
Outputs:
- leaf_sol: float32 [131072, 256], P(('subtree', 'fshard'), 'chan')
- node_sol: float32 [32768, 256], P(('subtree', 'fshard'), 'chan')
The draws below stay inside these ranges and needn't reach their ends.
Inputs may be any that keep to these rules, and one draw needn't show every extreme that they name: `leaf_rows`: each row holds 512 distinct row numbers of the parents. `node_rows`: each row holds 512 distinct row numbers of the parent. `leaf_inv`: each node's 4096 x 4096 block is lower triangular with diagonal entries between 0.6 and 1.4. `node_inv`: each node's 1024 x 1024 block is lower triangular with diagonal entries between 0.6 and 1.4.
All inputs are finite; a program needn't handle non-finite values.
Results may differ from the reference program's by a relative error of at most 0.0003.
Values sent between devices are 32-bit elements; how exact they have to be, the bound alone decides.
No kernel may reach another device: no remote copies, remote signals or barrier semaphores. Data moves between devices by JAX's collectives and lax.ppermute only.
A program may use at most 128 MiB of HBM per device.

```python
import jax
import jax.numpy as jnp
from jax import lax

CH = 256
LEAF = 4096
SEP = 1024
UPD = 512
DEPTH = 5
N_SUBTREE = 32


def lower_blocks(offdiag, diagonal, order):
    rows = (jnp.arange(offdiag.shape[0], dtype=jnp.int32) % order)[:, None]
    cols = jnp.arange(order, dtype=jnp.int32)[None, :]
    return jnp.where(cols < rows, offdiag, jnp.where(cols == rows, diagonal, 0.0))


def row_blocks(key, count, order, taken):
    keys = jax.random.split(key, count)
    perms = jax.vmap(lambda single: jax.random.permutation(single, order))(keys)
    return perms[:, :taken].astype(jnp.int32)


def draw_leaf_inv(key, part):
    key = jax.random.fold_in(key, 31)
    first, second = jax.random.split(key)
    shape = (N_SUBTREE * LEAF, LEAF)
    offdiag = jax.random.truncated_normal(first, -4.0, 4.0, shape, jnp.float32)
    diagonal = jax.random.uniform(second, (N_SUBTREE * LEAF, 1), jnp.float32, 0.6, 1.4)
    return lower_blocks(offdiag * (0.5 / LEAF ** 0.5), diagonal, LEAF)


def draw_node_inv(key, part):
    key = jax.random.fold_in(key, 37)
    first, second = jax.random.split(key)
    shape = (N_SUBTREE * SEP, SEP)
    offdiag = jax.random.truncated_normal(first, -4.0, 4.0, shape, jnp.float32)
    diagonal = jax.random.uniform(second, (N_SUBTREE * SEP, 1), jnp.float32, 0.6, 1.4)
    return lower_blocks(offdiag * (0.5 / SEP ** 0.5), diagonal, SEP)


def draw_leaf_rows(key, part):
    key = jax.random.fold_in(key, 41)
    return row_blocks(key, N_SUBTREE, SEP, UPD)


def draw_node_rows(key, part):
    key = jax.random.fold_in(key, 43)
    return row_blocks(key, N_SUBTREE, SEP, UPD)


def levels(own_key, extent, pieces, least, high):
    loudness = 1.0
    for position, parts in pieces:
        steps = jax.random.uniform(jax.random.fold_in(jax.random.fold_in(own_key, 6), position), (parts,), jnp.float32, least / len(pieces), high / len(pieces))
        loudness = loudness * jnp.repeat(jnp.exp(steps), extent[position] // parts).reshape((-1,) + (1,) * (len(extent) - 1 - position))
    return loudness


def normal_values(key, dims, spread, bound, shards=(), held_as=jnp.bfloat16):
    level = levels(key, dims, shards, -0.22, 0.18) if shards else 1.0
    result = jax.random.normal(key, dims, jnp.float32) * spread * level
    return jnp.minimum(jnp.maximum(result, -bound), bound).astype(held_as)


def setup_inputs(seed: int = 0) -> dict:
    key_of = jax.random.split(jax.random.key(seed), 9)
    leaf_rhs = normal_values(key_of[0], (N_SUBTREE * LEAF, CH), 1.0, 6.0, ((0, 64), (1, 2)), jnp.float32)
    node_rhs = normal_values(key_of[1], (N_SUBTREE * SEP, CH), 1.0, 6.0, ((0, 64), (1, 2)), jnp.float32)
    leaf_inv = draw_leaf_inv(jax.random.fold_in(key_of[8], 71), 0)
    node_inv = draw_node_inv(jax.random.fold_in(key_of[8], 71), 0)
    leaf_panel = normal_values(key_of[4], (N_SUBTREE * UPD, LEAF), (4 * LEAF) ** -0.5, 0.046875, ((0, 32), (1, 2)), jnp.float32)
    node_panel = normal_values(key_of[5], (N_SUBTREE * UPD, SEP), (4 * SEP) ** -0.5, 0.09375, ((0, 32), (1, 2)), jnp.float32)
    leaf_rows = draw_leaf_rows(jax.random.fold_in(key_of[8], 71), 0)
    node_rows = draw_node_rows(jax.random.fold_in(key_of[8], 71), 0)
    return dict(leaf_rhs=leaf_rhs, node_rhs=node_rhs, leaf_inv=leaf_inv, node_inv=node_inv, leaf_panel=leaf_panel, node_panel=node_panel, leaf_rows=leaf_rows, node_rows=node_rows)


HIGH = lax.Precision.HIGHEST
EPS = 1e-06

def level_of(place):
    level = 1
    value = place
    while value % 2 == 1 and level <= DEPTH:
        value = value // 2
        level = level + 1
    return level

def parent_of(place, level):
    reach = 2 ** (level - 1)
    if place >> level & 1 == 1:
        return place - reach
    return place + reach

def matmul(left, right):
    return jnp.dot(left, right, precision=HIGH, preferred_element_type=jnp.float32)

def normalize(field):
    scale = jnp.sqrt(lax.optimization_barrier(jnp.mean(field * field, axis=-1, keepdims=True)) + EPS)
    return field / scale

def reference(leaf_rhs, node_rhs, leaf_inv, node_inv, leaf_panel, node_panel, leaf_rows, node_rows):
    count = N_SUBTREE
    width = leaf_rhs.shape[1]
    half = UPD // 2
    rhs_leaf = leaf_rhs.reshape(count, LEAF, width)
    inv_leaf = leaf_inv.reshape(count, LEAF, LEAF)
    panel_leaf = leaf_panel.reshape(count, UPD, LEAF)
    rhs_node = node_rhs.reshape(count, SEP, width)
    inv_node = node_inv.reshape(count, SEP, SEP)
    panel_node = node_panel.reshape(count, UPD, SEP)
    leaf_y = jnp.einsum('nij,njc->nic', inv_leaf, rhs_leaf, precision=HIGH)
    leaf_up = jnp.einsum('nuj,njc->nuc', panel_leaf, leaf_y, precision=HIGH)
    accum = [jnp.zeros((SEP, width), jnp.float32) for place in range(count)]
    for place in range(count):
        rows = leaf_rows[place]
        if place % 2 == 0:
            accum[place] = accum[place].at[rows].add(leaf_up[place])
        else:
            lower = place - 1
            upper = (place + 1) % count
            accum[lower] = accum[lower].at[rows[:half]].add(leaf_up[place][:half])
            accum[upper] = accum[upper].at[rows[half:]].add(leaf_up[place][half:])
    order = sorted(range(count), key=level_of)
    solved = [None] * count
    for place in order:
        value = matmul(inv_node[place], rhs_node[place] - accum[place])
        solved[place] = value
        level = level_of(place)
        if level <= DEPTH:
            target = parent_of(place, level)
            accum[target] = accum[target].at[node_rows[place]].add(matmul(panel_node[place], value))
    answer = [None] * count
    for place in reversed(order):
        level = level_of(place)
        rest = solved[place]
        if level <= DEPTH:
            target = parent_of(place, level)
            seen = jnp.take(answer[target], node_rows[place], axis=0)
            rest = rest - matmul(panel_node[place].T, seen)
        answer[place] = matmul(inv_node[place].T, rest)
    seen_list = []
    for place in range(count):
        rows = leaf_rows[place]
        if place % 2 == 0:
            seen_list.append(jnp.take(answer[place], rows, axis=0))
        else:
            first = jnp.take(answer[place - 1], rows[:half], axis=0)
            second = jnp.take(answer[(place + 1) % count], rows[half:], axis=0)
            seen_list.append(jnp.concatenate([first, second], axis=0))
    seen_leaf = jnp.stack(seen_list)
    rest_leaf = leaf_y - jnp.einsum('nuj,nuc->njc', panel_leaf, seen_leaf, precision=HIGH)
    leaf_x = jnp.einsum('nij,nic->njc', inv_leaf, rest_leaf, precision=HIGH)
    node_x = jnp.stack(answer)
    leaf_sol = normalize(leaf_x).reshape(count * LEAF, width)
    node_sol = normalize(node_x).reshape(count * SEP, width)
    return (leaf_sol, node_sol)
```

```python
import functools

import jax
import jax.numpy as jnp
from jax import lax
from jax.experimental import pallas as pl
from jax.experimental.pallas import tpu as pltpu
from jax.sharding import PartitionSpec as P

HIGH = lax.Precision.HIGH
EPS = 1e-06
F32 = jnp.float32
BF16 = jnp.bfloat16
TILE = 512


def dot(left, right):
    return jnp.dot(left, right, precision=HIGH, preferred_element_type=F32)


def dot_t(left, right):
    return lax.dot_general(
        left, right, (((0,), (0,)), ((), ())), precision=HIGH, preferred_element_type=F32
    )


def halves(value):
    high = value.astype(BF16)
    return high, (value - high.astype(F32)).astype(BF16)


def mm(left, right):
    return jnp.dot(left, right, preferred_element_type=F32)


def dot3(left, right):
    left_hi, left_lo = left
    right_hi, right_lo = right
    return mm(left_hi, right_hi) + (mm(left_hi, right_lo) + mm(left_lo, right_hi))


PARAMS = dict(vmem_limit_bytes=40 * 1024 * 1024)


def leaf_own(f, inv, rhs):
    rows, width = rhs.shape
    n = rows // TILE

    def body(f_ref, inv_ref, rhs_ref, out_ref):
        i, j = pl.program_id(0), pl.program_id(1)

        @pl.when(j == 0)
        def _():
            out_ref[...] = jnp.zeros_like(out_ref)

        @pl.when(j <= i)
        def _():
            piece = rhs_ref[pl.ds(pl.multiple_of(j * TILE, TILE), TILE), :]
            out_ref[...] += dot3(halves(inv_ref[...]), halves(piece))

    return pl.pallas_call(
        body,
        grid_spec=pltpu.PrefetchScalarGridSpec(
            num_scalar_prefetch=1,
            grid=(n, n),
            in_specs=[
                pl.BlockSpec((TILE, TILE), lambda i, j, f: (i, f[0] * n + jnp.minimum(i, j))),
                pl.BlockSpec((rows, width), lambda i, j, f: (0, 0)),
            ],
            out_specs=pl.BlockSpec((TILE, width), lambda i, j, f: (i, 0)),
        ),
        out_shape=jax.ShapeDtypeStruct((rows, width), F32),
        compiler_params=pltpu.CompilerParams(**PARAMS),
        cost_estimate=pl.CostEstimate(flops=4 * 10**9, bytes_accessed=12 * 2**20, transcendentals=0),
        name="leaf_own",
    )(f, inv, rhs)


def leaf_other(f, inv, piece, sofar, step):
    rows, width = sofar.shape
    depth = piece.shape[0]
    n = rows // TILE

    def body(f_ref, inv_ref, piece_ref, sofar_ref, out_ref):
        @pl.when(f_ref[0] == 0)
        def _():
            out_ref[...] = sofar_ref[...]

        @pl.when(f_ref[0] == 1)
        def _():
            out_ref[...] = sofar_ref[...] + dot3(halves(inv_ref[...]), halves(piece_ref[...]))

    return pl.pallas_call(
        body,
        grid_spec=pltpu.PrefetchScalarGridSpec(
            num_scalar_prefetch=1,
            grid=(n,),
            in_specs=[
                pl.BlockSpec((TILE, depth), lambda i, f: (i * f[0], step * f[0])),
                pl.BlockSpec((depth, width), lambda i, f: (0, 0)),
                pl.BlockSpec((TILE, width), lambda i, f: (i, 0)),
            ],
            out_specs=pl.BlockSpec((TILE, width), lambda i, f: (i, 0)),
        ),
        out_shape=jax.ShapeDtypeStruct((rows, width), F32),
        compiler_params=pltpu.CompilerParams(**PARAMS),
        cost_estimate=pl.CostEstimate(flops=10**9, bytes_accessed=5 * 2**20, transcendentals=0),
        name="leaf_other",
    )(f, inv, piece, sofar)


def leaf_back_own(f, inv, value):
    rows, width = value.shape
    n = rows // TILE

    def body(f_ref, inv_ref, value_ref, out_ref, total):
        j, i = pl.program_id(0), pl.program_id(1)

        @pl.when(i == 0)
        def _():
            total[...] = jnp.zeros_like(total)

        @pl.when(i >= j)
        def _():
            piece = value_ref[pl.ds(pl.multiple_of(i * TILE, TILE), TILE), :]
            total[...] += dot3(halves(piece.T), halves(inv_ref[...]))

        @pl.when(i == n - 1)
        def _():
            out_ref[...] = total[...].T

    return pl.pallas_call(
        body,
        grid_spec=pltpu.PrefetchScalarGridSpec(
            num_scalar_prefetch=1,
            grid=(n, n),
            in_specs=[
                pl.BlockSpec((TILE, TILE), lambda j, i, f: (jnp.maximum(i, j), f[0] * n + j)),
                pl.BlockSpec((rows, width), lambda j, i, f: (0, 0)),
            ],
            out_specs=pl.BlockSpec((TILE, width), lambda j, i, f: (j, 0)),
            scratch_shapes=[pltpu.VMEM((width, TILE), F32)],
        ),
        out_shape=jax.ShapeDtypeStruct((rows, width), F32),
        compiler_params=pltpu.CompilerParams(**PARAMS),
        cost_estimate=pl.CostEstimate(flops=4 * 10**9, bytes_accessed=12 * 2**20, transcendentals=0),
        name="leaf_back_own",
    )(f, inv, value)


def leaf_back_other(f, inv, value):
    rows, width = value.shape
    n = rows // TILE

    def body(f_ref, inv_ref, value_ref, out_ref, total):
        j, i = pl.program_id(0), pl.program_id(1)

        @pl.when(f_ref[0] == 1)
        def _():
            @pl.when(i == 0)
            def _():
                total[...] = jnp.zeros_like(total)

            piece = value_ref[pl.ds(pl.multiple_of(i * TILE, TILE), TILE), :]
            total[...] += dot3(halves(piece.T), halves(inv_ref[...]))

            @pl.when(i == n - 1)
            def _():
                out_ref[...] = total[...].T

        @pl.when((f_ref[0] == 0) & (i == n - 1))
        def _():
            out_ref[...] = jnp.zeros_like(out_ref)

    return pl.pallas_call(
        body,
        grid_spec=pltpu.PrefetchScalarGridSpec(
            num_scalar_prefetch=1,
            grid=(n, n),
            in_specs=[
                pl.BlockSpec((TILE, TILE), lambda j, i, f: (i * f[0], j * f[0])),
                pl.BlockSpec((rows, width), lambda j, i, f: (0, 0)),
            ],
            out_specs=pl.BlockSpec((TILE, width), lambda j, i, f: (j, 0)),
            scratch_shapes=[pltpu.VMEM((width, TILE), F32)],
        ),
        out_shape=jax.ShapeDtypeStruct((rows, width), F32),
        compiler_params=pltpu.CompilerParams(**PARAMS),
        cost_estimate=pl.CostEstimate(flops=6 * 10**9, bytes_accessed=18 * 2**20, transcendentals=0),
        name="leaf_back_other",
    )(f, inv, value)


def panel_own(f, panel, inv):
    upd, rows = panel.shape
    n = rows // TILE

    def body(f_ref, panel_ref, inv_ref, out_ref):
        j, i = pl.program_id(0), pl.program_id(1)

        @pl.when(i == 0)
        def _():
            out_ref[...] = jnp.zeros_like(out_ref)

        @pl.when(i >= j)
        def _():
            out_ref[...] += dot3(halves(panel_ref[...]), halves(inv_ref[...]))

    return pl.pallas_call(
        body,
        grid_spec=pltpu.PrefetchScalarGridSpec(
            num_scalar_prefetch=1,
            grid=(n, n),
            in_specs=[
                pl.BlockSpec((upd, TILE), lambda j, i, f: (0, jnp.maximum(i, j))),
                pl.BlockSpec((TILE, TILE), lambda j, i, f: (jnp.maximum(i, j), f[0] * n + j)),
            ],
            out_specs=pl.BlockSpec((upd, TILE), lambda j, i, f: (0, j)),
        ),
        out_shape=jax.ShapeDtypeStruct((upd, rows), F32),
        compiler_params=pltpu.CompilerParams(**PARAMS),
        cost_estimate=pl.CostEstimate(flops=8 * 10**9, bytes_accessed=20 * 2**20, transcendentals=0),
        name="panel_own",
    )(f, panel, inv)


def panel_other(fc, panel, inv):
    upd, rows = panel.shape
    half = upd // 2
    n = rows // TILE

    def body(f_ref, panel_ref, inv_ref, out_ref):
        i = pl.program_id(1)

        @pl.when(i == 0)
        def _():
            out_ref[...] = jnp.zeros_like(out_ref)

        @pl.when(f_ref[0] == 1)
        def _():
            out_ref[...] += dot3(halves(panel_ref[...]), halves(inv_ref[...]))

    return pl.pallas_call(
        body,
        grid_spec=pltpu.PrefetchScalarGridSpec(
            num_scalar_prefetch=1,
            grid=(n, n),
            in_specs=[
                pl.BlockSpec((half, TILE), lambda j, i, f: (f[1], i * f[0])),
                pl.BlockSpec((TILE, TILE), lambda j, i, f: (i * f[0], j * f[0])),
            ],
            out_specs=pl.BlockSpec((half, TILE), lambda j, i, f: (0, j)),
        ),
        out_shape=jax.ShapeDtypeStruct((half, rows), F32),
        compiler_params=pltpu.CompilerParams(**PARAMS),
        cost_estimate=pl.CostEstimate(flops=8 * 10**9, bytes_accessed=20 * 2**20, transcendentals=0),
        name="panel_other",
    )(fc, panel, inv)


def level_of(place, depth):
    level = 1
    while place % 2 == 1 and level <= depth:
        place //= 2
        level += 1
    return level


def on_device(leaf_rhs, node_rhs, leaf_inv, node_inv, leaf_panel, node_panel, leaf_rows, node_rows):
    count = lax.axis_size("subtree")
    depth = count.bit_length() - 1
    place = lax.axis_index("subtree")
    f = lax.axis_index("fshard").astype(jnp.int32)
    c = lax.axis_index("chan").astype(jnp.int32)
    low = f == 0
    f_arr = f[None]
    fc_arr = jnp.stack([f, c])
    width = leaf_rhs.shape[1]
    upd = leaf_rows.shape[1]
    half = upd // 2
    sep_half = node_rhs.shape[0]
    height = 2 * sep_half
    rows = leaf_rhs.shape[0]
    is_even = place % 2 == 0
    levels = [level_of(d, depth) for d in range(count)]
    axes = ("subtree", "fshard")

    def send(value, triples):
        return lax.ppermute(value, axes, [(2 * s + g, 2 * t + h) for s, g, t, h in triples])

    everyone = range(count)
    evens = range(0, count, 2)
    odds = range(1, count, 2)

    def after(value, *first):
        return lax.optimization_barrier((value,) + first)[0]

    up_left = [(d - 2 ** (levels[d] - 2), 1, d, 1) for d in odds]
    up_right = [(d + 2 ** (levels[d] - 2), 1, d, 1) for d in odds if levels[d] <= depth]
    leaf_left = [(o, 1, (o + 1) % count, 1) for o in odds]
    leaf_right = [(o, 1, o - 1, 1) for o in odds]
    def both(pairs):
        return [(s, g, t, g) for s, _, t, _ in pairs for g in (0, 1)]

    node_index, leaf_index = node_rows[0], leaf_rows[0]
    from_left = send(node_index, both(up_left))
    from_right = send(node_index, both(up_right))
    from_right = jnp.where(place == count - 1, -1, from_right)
    leaf_l = send(leaf_index[half:], both(leaf_left))
    leaf_r = send(leaf_index[:half], both(leaf_right))
    index = jnp.where(
        is_even,
        jnp.concatenate([leaf_index, leaf_l, leaf_r]),
        jnp.concatenate([from_left, from_right]),
    )
    chosen = (jnp.arange(height, dtype=jnp.int32)[:, None] == index[None, :]).astype(F32)

    part = dot(node_panel, node_inv)
    part_even = send(part[:, :sep_half], [(d, 0, d, 1) for d in evens])

    pieces = rows // TILE
    got = []
    last = part_even
    for k in range(pieces):
        got.append(send(leaf_rhs[k * TILE : (k + 1) * TILE], [(d, 0, d, 1) for d in everyone]))
    leaf_y = leaf_own(f_arr, leaf_inv, leaf_rhs)
    up_low = send(dot(leaf_panel, leaf_y), [(d, 0, d, 1) for d in everyone])
    rhs_low = send(node_rhs, [(d, 0, d, 1) for d in everyone])
    for k in range(pieces):
        leaf_y = leaf_other(f_arr, leaf_inv, got[k], leaf_y, k)
    leaf_up = dot(leaf_panel, leaf_y) + up_low

    part_odd = send(after(part[:, :sep_half], up_low), [(d, 0, d, 1) for d in odds])
    inv_low = send(after(node_inv[:, :sep_half], part_odd), [(d, 0, d, 1) for d in everyone])
    first_cols = part[:, :sep_half] + part_even + part_odd
    panel_inv = jnp.concatenate([first_cols, part[:, sep_half:]], axis=1)
    node_r = jnp.concatenate([rhs_low, node_rhs], axis=0)
    lift = dot(panel_inv, chosen)
    base_up = dot(panel_inv, node_r)

    inv_full = jnp.concatenate(
        [jnp.concatenate([inv_low, jnp.zeros_like(inv_low)], axis=1), node_inv], axis=0
    )
    inv_sel = dot(inv_full, chosen)
    inv_r = dot(inv_full, node_r)
    quad = dot_t(inv_sel, inv_sel)
    base_down = dot_t(inv_sel, inv_r)
    top = count - 1
    sub = (count // 2) - 1
    top_quad, top_base = (
        send(v, [(top, 1, sub, 1)]) for v in (quad[:upd, :upd], base_down[:upd])
    )

    from_l = send(leaf_up[half:], leaf_left)
    from_r = send(leaf_up[:half], leaf_right)
    child_up = jnp.concatenate([leaf_up, from_l, from_r], axis=0)
    all_up = jnp.where(is_even, child_up, 0.0)
    node_up = base_up - dot(lift, child_up)
    for level in range(2, depth + 1):
        at = [d for d in everyone if levels[d] == level]
        left = send(node_up, [t for t in up_left if t[2] in at])
        right = send(node_up, [t for t in up_right if t[2] in at])
        child_up = jnp.concatenate([left, right], axis=0)
        all_up = all_up + child_up
        node_up = base_up - dot(lift, child_up)
    seen = top_base - dot(top_quad, node_up)
    top_up = send(node_up, [(sub, 1, top, 1)])

    from_up = base_down - dot(quad, all_up)
    all_seen = seen
    for level in range(depth, 0, -1):
        at = [d for d in everyone if levels[d] == level]
        down = from_up - dot_t(lift, seen)
        if level >= 2:
            to_left = send(down[:upd], [(t, h, s, g) for s, g, t, h in up_left if t in at])
            to_right = send(down[upd:], [(t, h, s, g) for s, g, t, h in up_right if t in at])
            seen = to_left + to_right
            all_seen = all_seen + seen
    own = send(down[:upd], [(e, 1, e, 0) for e in evens])
    to_left = send(down[upd + half :], [(e, 1, e + 1, 1) for e in evens])
    to_left0 = send(down[upd + half :], [(e, 1, e + 1, 0) for e in evens])
    to_right = send(down[upd : upd + half], [(e, 1, (e - 1) % count, 1) for e in evens])
    to_right0 = send(down[upd : upd + half], [(e, 1, (e - 1) % count, 0) for e in evens])
    leaf_seen = jnp.where(
        is_even,
        jnp.where(low, own, down[:upd]),
        jnp.concatenate([to_left + to_left0, to_right + to_right0], axis=0),
    )

    base_x = leaf_back_own(f_arr, leaf_inv, leaf_y)
    base_x = base_x + send(
        leaf_back_other(f_arr, leaf_inv, leaf_y), [(d, 1, d, 0) for d in everyone]
    )
    pan_own = panel_own(f_arr, leaf_panel, leaf_inv)
    pan_mine = send(panel_other(fc_arr, leaf_panel, leaf_inv), [(d, 1, d, 0) for d in everyone])
    pan_peer = lax.ppermute(pan_mine, ("chan", "fshard"), [(0, 2), (2, 0)])

    seen_mine = jnp.where(c == 0, leaf_seen[:half], leaf_seen[half:])
    seen_peer = jnp.where(c == 0, leaf_seen[half:], leaf_seen[:half])
    leaf_x = base_x - (
        dot_t(pan_own, leaf_seen) + dot_t(pan_mine, seen_mine) + dot_t(pan_peer, seen_peer)
    )

    tail_up = jnp.concatenate([top_up, jnp.zeros_like(top_up)], axis=0)
    node_y = inv_r - dot(inv_sel, all_up + tail_up)
    base_node = dot_t(inv_full, node_y)
    node_x = base_node - dot_t(panel_inv, all_seen)
    node_low = send(node_x[:sep_half], [(d, 1, d, 0) for d in everyone])
    node_x = jnp.where(low, node_low, node_x[sep_half:])

    squares = jnp.concatenate([jnp.sum(leaf_x * leaf_x, axis=1), jnp.sum(node_x * node_x, axis=1)])
    squares = squares + lax.ppermute(squares, "chan", [(0, 1), (1, 0)])
    channels = width * lax.axis_size("chan")
    scale = jnp.sqrt(squares / channels + EPS)[:, None]
    return (leaf_x / scale[:rows], node_x / scale[rows:])


def solution(mesh):
    in_specs = (
        P(("subtree", "fshard"), "chan"),
        P(("subtree", "fshard"), "chan"),
        P(("subtree", "fshard"), None),
        P(("subtree", "fshard"), None),
        P("subtree", "fshard"),
        P("subtree", "fshard"),
        P("subtree", None),
        P("subtree", None),
    )
    out_specs = (P(("subtree", "fshard"), "chan"), P(("subtree", "fshard"), "chan"))
    return jax.shard_map(
        on_device, mesh=mesh, in_specs=in_specs, out_specs=out_specs, check_vma=False
    )
```

```python
import jax
import jax.numpy as jnp
from jax import lax
from jax.experimental import pallas as pl
from jax.experimental.pallas import tpu as pltpu
from jax.sharding import PartitionSpec as P

EPS = 1e-06
F32 = jnp.float32
BF16 = jnp.bfloat16
TILE = 512
MIB = 1024 * 1024


def halves(value):
    high = value.astype(BF16)
    return high, (value - high.astype(F32)).astype(BF16)


def mm(left, right):
    return jnp.dot(left, right, preferred_element_type=F32)


def wide(value):
    return jnp.concatenate(halves(value), axis=1)


def tall(value):
    return jnp.concatenate(halves(value), axis=0)


def times(split, right_wide):
    total = mm(split[0], right_wide) + mm(split[1], right_wide)
    width = total.shape[1] // 2
    return total[:, :width] + total[:, width:]


def under(left_tall, split):
    total = mm(left_tall, split[0]) + mm(left_tall, split[1])
    height = total.shape[0] // 2
    return total[:height] + total[height:]


def dot3(left, right):
    return mm(left[0], right[0]) + (mm(left[0], right[1]) + mm(left[1], right[0]))


def exact(split, chosen):
    return mm(split[0], chosen) + mm(split[1], chosen)


def selection(index_row, height):
    rows = lax.broadcasted_iota(jnp.int32, (height, index_row.shape[1]), 0)
    return (rows == index_row).astype(F32).astype(BF16)


ANY = pl.BlockSpec(memory_space=pl.ANY)
SMEM = pl.BlockSpec(memory_space=pltpu.SMEM)
VMEM = pl.BlockSpec(memory_space=pltpu.VMEM)


def cost(mflop, mib):
    return pl.CostEstimate(flops=mflop * 10**6, bytes_accessed=mib * 1024, transcendentals=0)


def call(body, name, scalars, ins, deps, outs, aliases=None, vmem=24, mflop=500, mib=4):
    n_in, n_dep = len(ins), len(deps)

    def kernel(*refs):
        body(refs[0], *refs[1 : 1 + n_in], *refs[1 + n_in + n_dep :])

    return pl.pallas_call(
        kernel,
        in_specs=[SMEM] + [VMEM] * n_in + [ANY] * n_dep,
        out_specs=[VMEM] * len(outs),
        out_shape=[jax.ShapeDtypeStruct(s, t) for s, t in outs],
        input_output_aliases=aliases or {},
        compiler_params=pltpu.CompilerParams(vmem_limit_bytes=vmem * MIB),
        cost_estimate=cost(mflop, mib),
        name=name,
    )(scalars, *ins, *deps)


def tiled(body, name, scalars, grid, ins, deps, outs, scratch=(), aliases=None, vmem=28, mflop=4000, mib=12):
    n_in, n_dep = len(ins), len(deps)
    n_s = len(scalars)

    def kernel(*refs):
        body(*refs[: n_s + n_in], *refs[n_s + n_in + n_dep :])

    return pl.pallas_call(
        kernel,
        grid_spec=pltpu.PrefetchScalarGridSpec(
            num_scalar_prefetch=n_s,
            grid=grid,
            in_specs=[pl.BlockSpec(b, m) for _, b, m in ins] + [ANY] * n_dep,
            out_specs=[pl.BlockSpec(b, m) for _, b, m in outs],
            scratch_shapes=list(scratch),
        ),
        out_shape=[jax.ShapeDtypeStruct(s, F32) for s, _, _ in outs],
        input_output_aliases=aliases or {},
        compiler_params=pltpu.CompilerParams(vmem_limit_bytes=vmem * MIB),
        cost_estimate=cost(mflop, mib),
        name=name,
    )(*scalars, *[v for v, _, _ in ins], *deps)


def rows_of(ref, block, size=TILE):
    return ref[pl.ds(pl.multiple_of(block * size, size), size), :]


def leaf_own(sc, inv, rhs, panel, deps):
    rows, width = rhs.shape
    upd = panel.shape[0]
    tile = 2 * TILE
    n = rows // tile
    steps = [(i, j) for i in range(n) for j in range(i + 1)]
    at_i = jnp.array([i for i, _ in steps], jnp.int32)
    at_j = jnp.array([j for _, j in steps], jnp.int32)

    def body(sc, ti, tj, inv_ref, rhs_ref, panel_ref, y_ref, up_ref, rhs_wide):
        s = pl.program_id(0)
        i, j = ti[s], tj[s]

        @pl.when(s == 0)
        def _():
            rhs_wide[...] = wide(rhs_ref[...])
            up_ref[...] = jnp.zeros_like(up_ref)

        value = times(halves(inv_ref[...]), rows_of(rhs_wide, j, tile))

        @pl.when(j == 0)
        def _():
            y_ref[...] = value

        @pl.when(j > 0)
        def _():
            y_ref[...] += value

        @pl.when((j == i) & (sc[0] == 0))
        def _():
            up_ref[...] += times(halves(panel_ref[...]), wide(y_ref[...]))

    return tiled(
        body, "leaf_own", (sc, at_i, at_j), (len(steps),),
        [
            (inv, (tile, tile), lambda s, sc, ti, tj: (ti[s], sc[0] * n + tj[s])),
            (rhs, (rows, width), lambda s, *_: (0, 0)),
            (panel, (upd, tile), lambda s, sc, ti, tj: (0, ti[s])),
        ],
        deps,
        [
            ((rows, width), (tile, width), lambda s, sc, ti, tj: (ti[s], 0)),
            ((upd, width), (upd, width), lambda s, *_: (0, 0)),
        ],
        vmem=40,
        scratch=[pltpu.VMEM((rows, 2 * width), BF16)],
    )


def leaf_other(sc, inv, piece, y, step, panel, deps):
    rows, width = y.shape
    depth = piece.shape[0]
    tile = 2 * TILE
    whole = lambda i, sc: (0, 0)
    ins = [
        (inv, (tile, depth), lambda i, sc: (i * sc[0], step * sc[0])),
        (piece, (depth, width), whole),
        (y, (tile, width), lambda i, sc: (i, 0)),
    ]
    outs = [((rows, width), (tile, width), lambda i, sc: (i, 0))]
    if panel is not None:
        upd = panel.shape[0]
        ins.append((panel, (upd, tile), lambda i, sc: (0, i * sc[0])))
        outs.append(((upd, width), (upd, width), whole))

    def body(sc, inv_ref, piece_ref, y_in, *rest):
        *rest, piece_wide = rest
        i = pl.program_id(0)

        @pl.when(i == 0)
        def _():
            piece_wide[...] = wide(piece_ref[...])

        if panel is None:
            (y_ref,) = rest
        else:
            panel_ref, y_ref, up_ref = rest

        @pl.when(sc[0] == 0)
        def _():
            y_ref[...] = y_in[...]

        @pl.when(sc[0] == 1)
        def _():
            value = y_in[...] + times(halves(inv_ref[...]), piece_wide[...])
            y_ref[...] = value
            if panel is not None:
                lift = times(halves(panel_ref[...]), wide(value))

                @pl.when(i == 0)
                def _():
                    up_ref[...] = lift

                @pl.when(i > 0)
                def _():
                    up_ref[...] += lift

    return tiled(
        body, "leaf_other", (sc,), (rows // tile,), ins, deps, outs,
        scratch=[pltpu.VMEM((depth, 2 * width), BF16)], mflop=6000, mib=12, vmem=40,
    )


def back_other(sc, inv, y, panel, first, deps):
    rows, width = y.shape
    upd = panel.shape[0]
    half = upd // 2

    def body(sc, panel_ref, y_ref, inv_ref, lift_ref, back_ref, hi_ref, lo_ref):
        @pl.when(sc[0] == 1)
        def _():
            @pl.when(pl.program_id(0) == 0)
            def _():
                hi_ref[:half, :], lo_ref[:half, :] = halves(panel_ref[...])
                hi_ref[half:, :], lo_ref[half:, :] = halves(y_ref[...].T)

            value = dot3((hi_ref[...], lo_ref[...]), halves(inv_ref[...]))
            lift_ref[...] = value[:half]
            back_ref[...] = value[half:]

    return tiled(
        body, "back_other", (sc,), (2,),
        [
            (panel, (half, rows), lambda j, sc: (sc[1] * sc[0], 0)),
            (y, (rows, width), lambda j, sc: (0, 0)),
            (inv, (rows, TILE), lambda j, sc: (0, (first + j) * sc[0])),
        ],
        deps,
        [
            ((half, 2 * TILE), (half, TILE), lambda j, sc: (0, j)),
            ((width, 2 * TILE), (width, TILE), lambda j, sc: (0, j)),
        ],
        scratch=[pltpu.VMEM((half + width, rows), BF16)] * 2,
        mflop=4000, mib=12, vmem=40,
    )


def back_own(sc, inv, y, panel, columns, deps):
    rows, width = y.shape
    upd = panel.shape[0]
    n = rows // TILE
    steps = [(j, i) for j in columns for i in range(j, n)]
    at_j = jnp.array([j for j, _ in steps], jnp.int32)
    at_i = jnp.array([i for _, i in steps], jnp.int32)
    base = columns[0]

    def body(sc, tj, ti, y_ref, panel_ref, inv_ref, out_ref):
        s = pl.program_id(0)
        block = halves(inv_ref[...])
        back = under(tall(y_ref[...].T), block)
        lift = dot3(halves(panel_ref[...]), block)

        @pl.when(ti[s] == tj[s])
        def _():
            out_ref[:width, :] = back
            out_ref[width:, :] = lift

        @pl.when(ti[s] > tj[s])
        def _():
            out_ref[:width, :] += back
            out_ref[width:, :] += lift

    return tiled(
        body, "back_own", (sc, at_j, at_i), (len(steps),),
        [
            (y, (TILE, width), lambda s, sc, tj, ti: (ti[s], 0)),
            (panel, (upd, TILE), lambda s, sc, tj, ti: (0, ti[s])),
            (inv, (TILE, TILE), lambda s, sc, tj, ti: (ti[s], sc[0] * n + tj[s])),
        ],
        deps,
        [
            (
                (width + upd, TILE * len(columns)),
                (width + upd, TILE),
                lambda s, sc, tj, ti: (0, tj[s] - base),
            )
        ],
        mflop=1000 * len(steps), mib=2 * len(steps),
    )[0]


def leaf_tail(sc, own, mine, peer, back, seen, node, deps):
    half, width = seen[2].shape
    sep_half = node[0].shape[1]
    n = len(own)

    def body(sc, *refs):
        own_refs, mine_refs, peer_refs = refs[:n], refs[n : n + 2], refs[n + 2 : n + 4]
        back_refs, seen_refs, node_refs = refs[n + 4 : n + 6], refs[n + 6 : n + 12], refs[n + 12 : n + 14]
        x_ref, node_ref, squares_ref = refs[n + 14 :]
        is_low = sc[0] == 0
        whole = jnp.where(is_low, seen_refs[0][...], seen_refs[1][...])
        parts = jnp.concatenate(
            [seen_refs[2][...] + seen_refs[3][...], seen_refs[4][...] + seen_refs[5][...]], axis=0
        )
        seen_tall = tall(jnp.where(sc[2] % 2 == 0, whole, parts).T)
        first = sc[1] == 0
        col = 0
        for own_ref in own_refs:
            for at in range(0, own_ref.shape[1], TILE):
                which, inner = col // 2, (col % 2) * TILE
                cols, take = slice(at, at + TILE), slice(inner, inner + TILE)
                m, p = mine_refs[which][:, take], peer_refs[which][:, take]
                lift = own_ref[width:, cols] + jnp.concatenate(
                    [jnp.where(first, m, p), jnp.where(first, p, m)], axis=0
                )
                base = own_ref[:width, cols] + back_refs[which][:, take]
                x = base - under(seen_tall, halves(lift))
                out = slice(col * TILE, (col + 1) * TILE)
                x_ref[:, out] = x
                squares_ref[:, out] = jnp.sum(x * x, axis=0, keepdims=True)
                col += 1
        node_x = jnp.where(is_low, node_refs[0][...], node_refs[1][...])
        node_ref[...] = node_x
        squares_ref[:, col * TILE :] = jnp.sum(node_x * node_x, axis=0, keepdims=True)

    total = sum(v.shape[1] for v in own)
    return call(
        body, "leaf_tail", sc, [*own, *mine, *peer, *back, *seen, *node], deps,
        [((width, total), F32), ((width, sep_half), F32), ((1, total + sep_half), F32)],
        vmem=40, mflop=1000, mib=14,
    )


def node_part(sc, panel, inv, deps):
    upd = panel.shape[0]
    half = upd // 2
    cols = inv.shape[1]

    def body(sc, panel_ref, inv_ref, part_ref, half_ref):
        left = halves(panel_ref[...])
        for at in range(0, cols, TILE):
            part_ref[:, at : at + TILE] = dot3(left, halves(inv_ref[:, at : at + TILE]))
        half_ref[...] = part_ref[pl.ds(pl.multiple_of(sc[1] * half, half), half), :TILE]

    return call(
        body, "node_part", sc, [panel, inv], deps,
        [((upd, cols), F32), ((half, TILE), F32)], mflop=3000, mib=6,
    )


def node_lift(sc, part, mine, peer, rhs_low, rhs, index, deps):
    upd, cols = part.shape
    half = upd // 2
    width = rhs.shape[1]
    shapes = [
        ((upd, cols), BF16), ((upd, cols), BF16), ((cols, upd), BF16), ((cols, upd), BF16),
        ((upd, cols), F32), ((upd, width), F32),
    ]

    def body(sc, part_ref, mine_ref, peer_ref, low_ref, rhs_ref, index_ref, *rest):
        hi_ref, lo_ref, thi_ref, tlo_ref, whole_ref, base_ref = rest[-6:]

        @pl.when(sc[0] == 1)
        def _():
            first = sc[1] == 0
            m, p = mine_ref[...], peer_ref[...]
            whole_ref[...] = part_ref[...]
            whole_ref[:half, :TILE] += jnp.where(first, m, p)
            whole_ref[half:, :TILE] += jnp.where(first, p, m)
            split = halves(whole_ref[...])
            rhs_wide = jnp.concatenate([wide(low_ref[...]), wide(rhs_ref[...])], axis=0)
            base_ref[...] = times(split, rhs_wide)
            for at in range(0, cols, TILE):
                chosen = selection(index_ref[:, at : at + TILE], cols)
                value = exact(split, chosen)
                hi_ref[:, at : at + TILE], lo_ref[:, at : at + TILE] = halves(value)
                thi_ref[at : at + TILE, :], tlo_ref[at : at + TILE, :] = halves(value.T)

    ins = [part, mine, peer, rhs_low, rhs, index]
    return call(body, "node_lift", sc, ins, deps, shapes, vmem=40, mflop=4000, mib=12)


def node_top(sc, top, inv, rhs_low, rhs, index, deps):
    rows, cols = inv.shape
    width = rhs.shape[1]

    def body(sc, inv_ref, low_ref, rhs_ref, index_ref, out_ref):
        @pl.when(sc[2] == top)
        def _():
            split = halves(inv_ref[...])
            chosen = selection(index_ref[:, :TILE], cols)
            value = exact(split, chosen)
            own, low = wide(rhs_ref[...]), wide(low_ref[...])
            is_low = sc[0] == 0
            first = jnp.where(is_low, own.astype(F32), low.astype(F32)).astype(BF16)
            solved = times(split, jnp.concatenate([first, own], axis=0))
            left = halves(value.T)
            out_ref[:, :TILE] = dot3(left, halves(value))
            out_ref[:, TILE:] = dot3(left, halves(solved))

    return call(
        body, "node_top", sc, [inv, rhs_low, rhs, index], deps,
        [((TILE, TILE + width), F32)], mflop=2500, mib=5,
    )[0]


def node_select(sc, inv_low, inv, rhs_low, rhs, index, deps):
    rows, cols = inv.shape
    width = rhs.shape[1]

    def body(sc, inv_low_ref, inv_ref, low_ref, rhs_ref, index_ref, hi_ref, lo_ref, solved_ref):
        @pl.when(sc[0] == 1)
        def _():
            low_split, split = halves(inv_low_ref[...]), halves(inv_ref[...])
            low_wide = wide(low_ref[...])
            rhs_wide = jnp.concatenate([low_wide, wide(rhs_ref[...])], axis=0)
            solved_ref[:rows] = times(low_split, low_wide)
            solved_ref[rows:] = times(split, rhs_wide)
            for at in range(0, cols, TILE):
                chosen = selection(index_ref[:, at : at + TILE], cols)
                there = slice(at, at + TILE)
                hi_ref[:rows, there], lo_ref[:rows, there] = halves(exact(low_split, chosen[:rows]))
                hi_ref[rows:, there], lo_ref[rows:, there] = halves(exact(split, chosen))

    return call(
        body, "node_select", sc, [inv_low, inv, rhs_low, rhs, index], deps,
        [((cols, cols), BF16), ((cols, cols), BF16), ((cols, width), F32)],
        vmem=36, mflop=4000, mib=9,
    )


def climb(sc, level, base, hi, lo, pieces, kept, deps):
    upd, width = base.shape
    cols = hi.shape[1]
    n = len(pieces)

    def body(sc, base_ref, hi_ref, lo_ref, *refs):
        up_ref, kept_ref = refs[-2:]

        @pl.when((sc[0] == 1) & (sc[3] == level))
        def _():
            value = jnp.concatenate([r[...] for r in refs[:n]], axis=0)
            kept_ref[...] = value
            up_ref[...] = base_ref[...] - times((hi_ref[...], lo_ref[...]), wide(value))

    ins = [base, hi, lo, *pieces]
    aliases = None
    if kept is not None:
        aliases = {1 + len(ins): 1}
        ins = ins + [kept]
    return call(
        body, "climb", sc, ins, deps, [((upd, width), F32), ((cols, width), F32)],
        aliases=aliases, mflop=400, mib=3,
    )


def turn(sc, level, base, hi, lo, pieces, kept, top, inv_hi, inv_lo, solved, thi, tlo, deps):
    upd, width = base.shape
    cols = hi.shape[1]

    def body(sc, base_ref, hi_ref, lo_ref, l_ref, r_ref, kept_ref, top_a, top_b, ih_ref, il_ref,
             solved_ref, thi_ref, tlo_ref, up_ref, seen_ref, y_ref, from_up_ref, down_ref):
        is_top = sc[3] == level

        @pl.when(sc[0] == 1)
        def _():
            arrived = jnp.concatenate([l_ref[...], r_ref[...]], axis=0)
            u_wide = wide(jnp.where(is_top, arrived, kept_ref[...]))
            split = (ih_ref[...], il_ref[...])
            y = solved_ref[...] - times(split, u_wide)
            y_ref[...] = y
            from_up = under(tall(y.T), split).T
            from_up_ref[...] = from_up

            @pl.when(is_top)
            def _():
                up = base_ref[...] - times((hi_ref[...], lo_ref[...]), u_wide)
                up_ref[...] = up
                both = top_a[...] + top_b[...]
                seen = both[:, upd:] - times(halves(both[:, :upd]), wide(up))
                seen_ref[...] = seen
                down_ref[...] = from_up - times((thi_ref[...], tlo_ref[...]), wide(seen))

    return call(
        body, "turn", sc,
        [base, hi, lo, *pieces, kept, *top, inv_hi, inv_lo, solved, thi, tlo], deps,
        [((upd, width), F32), ((upd, width), F32), ((cols, width), F32), ((cols, width), F32),
         ((cols, width), F32)],
        vmem=36, mflop=1500, mib=12,
    )


def descend(sc, level, from_up, thi, tlo, pieces, kept, cuts, deps):
    cols, width = from_up.shape
    upd = kept.shape[0]
    n = len(pieces)

    def body(sc, from_ref, thi_ref, tlo_ref, *refs):
        outs = refs[n + 1 :]
        seen_ref = outs[0]

        @pl.when((sc[0] == 1) & (sc[3] == level))
        def _():
            value = refs[0][...]
            for ref in refs[1:n]:
                value += ref[...]
            seen_ref[...] = value
            z_wide = wide(value)
            at = 0
            for out in outs[1:]:
                size = out.shape[0]
                there = slice(at, at + size)
                out[...] = from_ref[there] - times((thi_ref[there], tlo_ref[there]), z_wide)
                at += size

    ins = [from_up, thi, tlo, *pieces, kept]
    return call(
        body, "descend", sc, ins, deps,
        [((upd, width), F32)] + [((size, width), F32) for size in cuts],
        aliases={len(ins): 0}, mflop=400, mib=3,
    )


def node_tail(sc, top, inv_low, inv, y, whole, seen, top_up, inv_hi, inv_lo, solved, deps):
    rows, cols = inv.shape
    width = y.shape[1]

    def body(sc, inv_low_ref, inv_ref, y_ref, whole_ref, seen_ref, up_ref, ih_ref, il_ref,
             solved_ref, low_ref, high_ref):
        def give(y, x):
            y_tall = tall(y.T)
            low_tall, high_tall = y_tall[:, :rows], y_tall[:, rows:]
            high_ref[...] = x[:, rows:] + under(high_tall, halves(inv_ref[:, rows:]))
            low_ref[...] = (
                x[:, :rows]
                + under(high_tall, halves(inv_ref[:, :rows]))
                + under(low_tall, halves(inv_low_ref[...]))
            )

        @pl.when((sc[0] == 1) & (sc[2] != top))
        def _():
            give(y_ref[...], -under(tall(seen_ref[...].T), halves(whole_ref[...])))

        @pl.when((sc[0] == 1) & (sc[2] == top))
        def _():
            split = (ih_ref[:, :TILE], il_ref[:, :TILE])
            give(solved_ref[...] - times(split, wide(up_ref[...])), jnp.zeros((width, cols), F32))

    return call(
        body, "node_tail", sc,
        [inv_low, inv, y, whole, seen, top_up, inv_hi, inv_lo, solved], deps,
        [((width, rows), F32), ((width, cols - rows), F32)], vmem=40, mflop=1500, mib=12,
    )


def finish(sc, leaf, node, squares, others, channels):
    width, rows = leaf.shape
    node_rows = node.shape[1]

    def body(sc, leaf_ref, node_ref, squares_ref, others_ref, leaf_out, node_out):
        scale = lax.rsqrt((squares_ref[...] + others_ref[...]) / channels + EPS)
        for at in range(0, rows, TILE):
            there = slice(at, at + TILE)
            leaf_out[there, :] = (leaf_ref[:, there] * scale[:, there]).T
        node_out[...] = (node_ref[...] * scale[:, rows:]).T

    return call(
        body, "finish", sc, [leaf, node, squares, others], [],
        [((rows, width), F32), ((node_rows, width), F32)], mflop=10, mib=3,
    )


def level_of(place, depth):
    level = 1
    while place % 2 == 1 and level <= depth:
        place //= 2
        level += 1
    return level


def after(value, *first):
    return lax.optimization_barrier((value,) + first)[0]


def on_device(leaf_rhs, node_rhs, leaf_inv, node_inv, leaf_panel, node_panel, leaf_rows, node_rows):
    count = lax.axis_size("subtree")
    depth = count.bit_length() - 1
    place = lax.axis_index("subtree").astype(jnp.int32)
    f = lax.axis_index("fshard").astype(jnp.int32)
    c = lax.axis_index("chan").astype(jnp.int32)
    level = jnp.ones((), jnp.int32)
    for bit in range(depth):
        level = level + ((place + 1) % 2 ** (bit + 1) == 0).astype(jnp.int32)
    sc = jnp.stack([f, c, place, level])
    low = f == 0
    is_even = place % 2 == 0
    width = leaf_rhs.shape[1]
    upd = leaf_rows.shape[1]
    half = upd // 2
    sep_half = node_rhs.shape[0]
    rows = leaf_rhs.shape[0]
    levels = [level_of(d, depth) for d in range(count)]
    everyone = range(count)
    evens, odds = range(0, count, 2), range(1, count, 2)
    top, sub = count - 1, count // 2 - 1

    def send(value, quads):
        pairs = [(2 * s + g, 2 * t + h) for s, g, t, h in quads]
        return lax.ppermute(value, ("subtree", "fshard"), pairs)

    def lift_over(value, places):
        return send(value, [(d, 0, d, 1) for d in places])

    def drop_over(value):
        return send(value, [(d, 1, d, 0) for d in everyone])

    def swap_chan(value, g):
        return lax.ppermute(value, ("chan", "fshard"), [(g, 2 + g), (2 + g, g)])

    left_kid = [(d - 2 ** (levels[d] - 2), d) for d in odds]
    right_kid = [(d + 2 ** (levels[d] - 2), d) for d in odds if levels[d] <= depth]

    piece_rows = rows // 2
    piece0 = lift_over(leaf_rhs[:piece_rows], everyone)
    part, part_half = node_part(sc, node_panel, node_inv, [])
    mine = lift_over(part_half, everyone)
    leaf_y, leaf_up = leaf_own(sc, leaf_inv, leaf_rhs, leaf_panel, [part])
    piece1 = lift_over(after(leaf_rhs[piece_rows:], piece0, leaf_up), everyone)
    up_low = lift_over(after(leaf_up, piece0), everyone)
    rhs_low = lift_over(after(node_rhs, piece0, leaf_up), everyone)
    y1 = leaf_other(sc, leaf_inv, piece0, leaf_y, 0, None, [leaf_up])[0]
    peer = swap_chan(after(mine, y1), 1)

    leaf_over = [(o, 1, (o + 1) % count, 1) for o in odds]
    leaf_under = [(o, 1, o - 1, 1) for o in odds]
    node_index, leaf_index = after((node_rows, leaf_rows), y1)
    leaf_l = send(leaf_index[:, half:], leaf_over)
    leaf_r = send(leaf_index[:, :half], leaf_under)
    from_left = send(node_index, [(s, g, t, g) for s, t in left_kid for g in (0, 1)])
    from_right = send(node_index, [(s, 1, t, 1) for s, t in right_kid])
    index = jnp.where(
        is_even,
        jnp.concatenate([leaf_index, leaf_l, leaf_r], axis=1),
        jnp.concatenate([from_left, jnp.where(place == top, -1, from_right)], axis=1),
    )

    leaf_y, leaf_up = leaf_other(sc, leaf_inv, piece1, y1, 1, leaf_panel, [])
    leaf_up = leaf_up + up_low
    inv_low = lift_over(after(node_inv[:, :sep_half], up_low, rhs_low, peer), everyone)

    from_l = send(leaf_up[half:], leaf_over)
    from_r = send(leaf_up[:half], leaf_under)
    hi, lo, thi, tlo, whole, base_up = node_lift(
        sc, part, mine, peer, rhs_low, node_rhs, index, [leaf_up]
    )
    node_up, kept = climb(sc, 1, base_up, hi, lo, [leaf_up, from_l, from_r], None, [])

    def edges(kid, at):
        pairs = [(s, t) for s, t in kid if levels[t] == at]
        return [(s, 1, t, 1) for s, t in pairs] + [(t, 1, s, 1) for s, t in pairs]

    def rise(value, at):
        return [
            send(value, edges(kid, at)) for kid in (left_kid, right_kid)
        ]

    got = rise(node_up, 2)
    pan0, back0 = back_other(sc, leaf_inv, leaf_y, leaf_panel, 0, [node_up])
    pan_mine0 = drop_over(pan0)
    pan_peer0 = swap_chan(pan_mine0, 0)
    top_part = node_top(sc, top, node_inv, rhs_low, node_rhs, index, [back0])
    tops = [send(top_part, [(top, g, sub, 1)]) for g in (0, 1)]
    node_up, kept = climb(sc, 2, base_up, hi, lo, got, kept, [top_part])
    got = rise(node_up, 3)
    pan1, back1 = back_other(sc, leaf_inv, leaf_y, leaf_panel, 2, [node_up])
    pan_mine1 = drop_over(pan1)
    pan_peer1 = swap_chan(pan_mine1, 0)
    back_mine0 = drop_over(after(back0, pan_mine1))
    back_mine1 = drop_over(after(back1, pan_mine1))
    node_up, kept = climb(sc, 3, base_up, hi, lo, got, kept, [back1])
    got = rise(node_up, 4)
    inv_hi, inv_lo, solved = node_select(sc, inv_low, node_inv, rhs_low, node_rhs, index, [node_up])
    node_up, kept = climb(sc, 4, base_up, hi, lo, got, kept, [inv_hi])
    got = rise(node_up, 5)
    own0 = back_own(sc, leaf_inv, leaf_y, leaf_panel, [0], [node_up])
    top_up, seen, node_y, from_up, down = turn(
        sc, depth, base_up, hi, lo, got, kept, tops, inv_hi, inv_lo, solved, thi, tlo, [own0]
    )
    late_up = send(top_up, [(sub, 1, top, 1)])

    def fall(left, right, at):
        return [
            send(v, edges(kid, at)) for v, kid in ((left, left_kid), (right, right_kid))
        ]

    got = fall(down[:upd], down[upd:], depth)
    own1 = back_own(sc, leaf_inv, leaf_y, leaf_panel, [1], [down])
    fill = [own1]
    for at in range(depth - 1, 1, -1):
        seen, left, right = descend(sc, at, from_up, thi, tlo, got, seen, (upd, upd), fill)
        got = fall(left, right, at)
        fill = []
        if at == depth - 1:
            own23 = back_own(sc, leaf_inv, leaf_y, leaf_panel, [2, 3], [left])
            fill = [own23]
    seen, mid, to_left, to_right = descend(
        sc, 1, from_up, thi, tlo, got, seen, (upd, half, half),
        [back_mine0, back_mine1, pan_peer0, pan_peer1],
    )
    seen_odd = [
        send(v, [(e, 1, (e + by) % count, g) for e in evens])
        for v, by in ((to_right, 1), (to_left, -1))
        for g in (1, 0)
    ]
    seen_own = send(mid, [(e, 1, e, 0) for e in evens])
    node_low, node_high = node_tail(
        sc, top, inv_low, node_inv, node_y, whole, seen, late_up, inv_hi, inv_lo, solved, [to_right]
    )
    leaf_x, node_x, squares = leaf_tail(
        sc, [own0, own1, own23], [pan_mine0, pan_mine1], [pan_peer0, pan_peer1],
        [back_mine0, back_mine1], [seen_own, mid, *seen_odd], [drop_over(after(node_low, seen_odd[0])), node_high], [],
    )
    others = lax.ppermute(squares, "chan", [(0, 1), (1, 0)])
    channels = float(width * lax.axis_size("chan"))
    return tuple(finish(sc, leaf_x, node_x, squares, others, channels))


def solution(mesh):
    in_specs = (
        P(("subtree", "fshard"), "chan"),
        P(("subtree", "fshard"), "chan"),
        P(("subtree", "fshard"), None),
        P(("subtree", "fshard"), None),
        P("subtree", "fshard"),
        P("subtree", "fshard"),
        P("subtree", None),
        P("subtree", None),
    )
    out_specs = (P(("subtree", "fshard"), "chan"), P(("subtree", "fshard"), "chan"))
    return jax.shard_map(
        on_device, mesh=mesh, in_specs=in_specs, out_specs=out_specs, check_vma=False
    )
```

```python
import jax
import jax.numpy as jnp
from jax import lax
from jax.experimental import pallas as pl
from jax.experimental.pallas import tpu as pltpu
from jax.sharding import PartitionSpec as P

EPS = 1e-06
F32 = jnp.float32
BF16 = jnp.bfloat16
TILE = 512
MIB = 1024 * 1024


def halves(value):
    high = value.astype(BF16)
    return high, (value - high.astype(F32)).astype(BF16)


def mm(left, right):
    return jnp.dot(left, right, preferred_element_type=F32)


def wide(value):
    return jnp.concatenate(halves(value), axis=1)


def tall(value):
    return jnp.concatenate(halves(value), axis=0)


def times(split, right_wide):
    total = mm(split[0], right_wide) + mm(split[1], right_wide)
    width = total.shape[1] // 2
    return total[:, :width] + total[:, width:]


def under(left_tall, split):
    total = mm(left_tall, split[0]) + mm(left_tall, split[1])
    height = total.shape[0] // 2
    return total[:height] + total[height:]


def dot3(left, right):
    return mm(left[0], right[0]) + (mm(left[0], right[1]) + mm(left[1], right[0]))


def exact(split, chosen):
    return mm(split[0], chosen) + mm(split[1], chosen)


def selection(index_row, height):
    rows = lax.broadcasted_iota(jnp.int32, (height, index_row.shape[1]), 0)
    return (rows == index_row).astype(F32).astype(BF16)


ANY = pl.BlockSpec(memory_space=pl.ANY)
SMEM = pl.BlockSpec(memory_space=pltpu.SMEM)
VMEM = pl.BlockSpec(memory_space=pltpu.VMEM)


def cost(mflop, mib):
    return pl.CostEstimate(flops=mflop * 10**6, bytes_accessed=mib * 1024, transcendentals=0)


def call(body, name, scalars, ins, deps, outs, aliases=None, vmem=24, mflop=500, mib=4):
    n_in, n_dep = len(ins), len(deps)

    def kernel(*refs):
        body(refs[0], *refs[1 : 1 + n_in], *refs[1 + n_in + n_dep :])

    return pl.pallas_call(
        kernel,
        in_specs=[SMEM] + [VMEM] * n_in + [ANY] * n_dep,
        out_specs=[VMEM] * len(outs),
        out_shape=[jax.ShapeDtypeStruct(s, t) for s, t in outs],
        input_output_aliases=aliases or {},
        compiler_params=pltpu.CompilerParams(vmem_limit_bytes=vmem * MIB),
        cost_estimate=cost(mflop, mib),
        name=name,
    )(scalars, *ins, *deps)


def tiled(body, name, scalars, grid, ins, deps, outs, scratch=(), aliases=None, vmem=28, mflop=4000, mib=12):
    n_in, n_dep = len(ins), len(deps)
    n_s = len(scalars)

    def kernel(*refs):
        body(*refs[: n_s + n_in], *refs[n_s + n_in + n_dep :])

    return pl.pallas_call(
        kernel,
        grid_spec=pltpu.PrefetchScalarGridSpec(
            num_scalar_prefetch=n_s,
            grid=grid,
            in_specs=[pl.BlockSpec(b, m) for _, b, m in ins] + [ANY] * n_dep,
            out_specs=[pl.BlockSpec(b, m) for _, b, m in outs],
            scratch_shapes=list(scratch),
        ),
        out_shape=[jax.ShapeDtypeStruct(s, F32) for s, _, _ in outs],
        input_output_aliases=aliases or {},
        compiler_params=pltpu.CompilerParams(vmem_limit_bytes=vmem * MIB),
        cost_estimate=cost(mflop, mib),
        name=name,
    )(*scalars, *[v for v, _, _ in ins], *deps)


def rows_of(ref, block, size=TILE):
    return ref[pl.ds(pl.multiple_of(block * size, size), size), :]


def leaf_own(sc, inv, rhs, panel, deps):
    rows, width = rhs.shape
    upd = panel.shape[0]
    tile = 2 * TILE
    n = rows // tile
    steps = [(i, j) for i in range(n) for j in range(i + 1)]
    at_i = jnp.array([i for i, _ in steps], jnp.int32)
    at_j = jnp.array([j for _, j in steps], jnp.int32)

    def body(sc, ti, tj, inv_ref, rhs_ref, panel_ref, y_ref, up_ref, rhs_wide):
        s = pl.program_id(0)
        i, j = ti[s], tj[s]

        @pl.when(s == 0)
        def _():
            rhs_wide[...] = wide(rhs_ref[...])
            up_ref[...] = jnp.zeros_like(up_ref)

        value = times(halves(inv_ref[...]), rows_of(rhs_wide, j, tile))

        @pl.when(j == 0)
        def _():
            y_ref[...] = value

        @pl.when(j > 0)
        def _():
            y_ref[...] += value

        @pl.when((j == i) & (sc[0] == 0))
        def _():
            up_ref[...] += times(halves(panel_ref[...]), wide(y_ref[...]))

    return tiled(
        body, "leaf_own", (sc, at_i, at_j), (len(steps),),
        [
            (inv, (tile, tile), lambda s, sc, ti, tj: (ti[s], sc[0] * n + tj[s])),
            (rhs, (rows, width), lambda s, *_: (0, 0)),
            (panel, (upd, tile), lambda s, sc, ti, tj: (0, ti[s])),
        ],
        deps,
        [
            ((rows, width), (tile, width), lambda s, sc, ti, tj: (ti[s], 0)),
            ((upd, width), (upd, width), lambda s, *_: (0, 0)),
        ],
        vmem=40,
        scratch=[pltpu.VMEM((rows, 2 * width), BF16)],
    )


def leaf_other(sc, inv, piece, y, step, panel, deps):
    rows, width = y.shape
    depth = piece.shape[0]
    tile = 2 * TILE
    whole = lambda i, sc: (0, 0)
    ins = [
        (inv, (tile, depth), lambda i, sc: (i * sc[0], step * sc[0])),
        (piece, (depth, width), whole),
        (y, (tile, width), lambda i, sc: (i, 0)),
    ]
    outs = [((rows, width), (tile, width), lambda i, sc: (i, 0))]
    if panel is not None:
        upd = panel.shape[0]
        ins.append((panel, (upd, tile), lambda i, sc: (0, i * sc[0])))
        outs.append(((upd, width), (upd, width), whole))

    def body(sc, inv_ref, piece_ref, y_in, *rest):
        *rest, piece_wide = rest
        i = pl.program_id(0)

        @pl.when(i == 0)
        def _():
            piece_wide[...] = wide(piece_ref[...])

        if panel is None:
            (y_ref,) = rest
        else:
            panel_ref, y_ref, up_ref = rest

        @pl.when(sc[0] == 0)
        def _():
            y_ref[...] = y_in[...]

        @pl.when(sc[0] == 1)
        def _():
            value = y_in[...] + times(halves(inv_ref[...]), piece_wide[...])
            y_ref[...] = value
            if panel is not None:
                lift = times(halves(panel_ref[...]), wide(value))

                @pl.when(i == 0)
                def _():
                    up_ref[...] = lift

                @pl.when(i > 0)
                def _():
                    up_ref[...] += lift

    return tiled(
        body, "leaf_other", (sc,), (rows // tile,), ins, deps, outs,
        scratch=[pltpu.VMEM((depth, 2 * width), BF16)], mflop=6000, mib=12, vmem=40,
    )


def back_other(sc, inv, y, panel, first, deps):
    rows, width = y.shape
    upd = panel.shape[0]
    half = upd // 2

    def body(sc, panel_ref, y_ref, inv_ref, lift_ref, back_ref, hi_ref, lo_ref):
        @pl.when(sc[0] == 1)
        def _():
            @pl.when(pl.program_id(0) == 0)
            def _():
                hi_ref[:half, :], lo_ref[:half, :] = halves(panel_ref[...])
                hi_ref[half:, :], lo_ref[half:, :] = halves(y_ref[...].T)

            value = dot3((hi_ref[...], lo_ref[...]), halves(inv_ref[...]))
            lift_ref[...] = value[:half]
            back_ref[...] = value[half:]

    return tiled(
        body, "back_other", (sc,), (2,),
        [
            (panel, (half, rows), lambda j, sc: (sc[1] * sc[0], 0)),
            (y, (rows, width), lambda j, sc: (0, 0)),
            (inv, (rows, TILE), lambda j, sc: (0, (first + j) * sc[0])),
        ],
        deps,
        [
            ((half, 2 * TILE), (half, TILE), lambda j, sc: (0, j)),
            ((width, 2 * TILE), (width, TILE), lambda j, sc: (0, j)),
        ],
        scratch=[pltpu.VMEM((half + width, rows), BF16)] * 2,
        mflop=4000, mib=12, vmem=32,
    )


def back_own(sc, inv, y, panel, columns, deps):
    rows, width = y.shape
    upd = panel.shape[0]
    n = rows // TILE
    steps = [(j, i) for j in columns for i in range(j, n)]
    at_j = jnp.array([j for j, _ in steps], jnp.int32)
    at_i = jnp.array([i for _, i in steps], jnp.int32)
    base = columns[0]

    def body(sc, tj, ti, y_ref, panel_ref, inv_ref, out_ref):
        s = pl.program_id(0)
        block = halves(inv_ref[...])
        back = under(tall(y_ref[...].T), block)
        lift = dot3(halves(panel_ref[...]), block)

        @pl.when(ti[s] == tj[s])
        def _():
            out_ref[:width, :] = back
            out_ref[width:, :] = lift

        @pl.when(ti[s] > tj[s])
        def _():
            out_ref[:width, :] += back
            out_ref[width:, :] += lift

    return tiled(
        body, "back_own", (sc, at_j, at_i), (len(steps),),
        [
            (y, (TILE, width), lambda s, sc, tj, ti: (ti[s], 0)),
            (panel, (upd, TILE), lambda s, sc, tj, ti: (0, ti[s])),
            (inv, (TILE, TILE), lambda s, sc, tj, ti: (ti[s], sc[0] * n + tj[s])),
        ],
        deps,
        [
            (
                (width + upd, TILE * len(columns)),
                (width + upd, TILE),
                lambda s, sc, tj, ti: (0, tj[s] - base),
            )
        ],
        mflop=1000 * len(steps), mib=2 * len(steps), vmem=18,
    )[0]


def leaf_tail(sc, own, mine, peer, back, seen, node, deps):
    half, width = seen[2].shape
    sep_half = node[0].shape[1]
    n = len(own)

    def body(sc, *refs):
        own_refs, mine_refs, peer_refs = refs[:n], refs[n : n + 2], refs[n + 2 : n + 4]
        back_refs, seen_refs, node_refs = refs[n + 4 : n + 6], refs[n + 6 : n + 12], refs[n + 12 : n + 14]
        x_ref, node_ref, squares_ref = refs[n + 14 :]
        is_low = sc[0] == 0
        whole = jnp.where(is_low, seen_refs[0][...], seen_refs[1][...])
        parts = jnp.concatenate(
            [seen_refs[2][...] + seen_refs[3][...], seen_refs[4][...] + seen_refs[5][...]], axis=0
        )
        seen_tall = tall(jnp.where(sc[2] % 2 == 0, whole, parts).T)
        first = sc[1] == 0
        col = 0
        for own_ref in own_refs:
            for at in range(0, own_ref.shape[1], TILE):
                which, inner = col // 2, (col % 2) * TILE
                cols, take = slice(at, at + TILE), slice(inner, inner + TILE)
                m, p = mine_refs[which][:, take], peer_refs[which][:, take]
                lift = own_ref[width:, cols] + jnp.concatenate(
                    [jnp.where(first, m, p), jnp.where(first, p, m)], axis=0
                )
                base = own_ref[:width, cols] + back_refs[which][:, take]
                x = base - under(seen_tall, halves(lift))
                out = slice(col * TILE, (col + 1) * TILE)
                x_ref[:, out] = x
                squares_ref[:, out] = jnp.sum(x * x, axis=0, keepdims=True)
                col += 1
        node_x = jnp.where(is_low, node_refs[0][...], node_refs[1][...])
        node_ref[...] = node_x
        squares_ref[:, col * TILE :] = jnp.sum(node_x * node_x, axis=0, keepdims=True)

    total = sum(v.shape[1] for v in own)
    return call(
        body, "leaf_tail", sc, [*own, *mine, *peer, *back, *seen, *node], deps,
        [((width, total), F32), ((width, sep_half), F32), ((1, total + sep_half), F32)],
        vmem=40, mflop=1000, mib=14,
    )


def node_part(sc, panel, inv, deps):
    upd = panel.shape[0]
    half = upd // 2
    cols = inv.shape[1]

    def body(sc, panel_ref, inv_ref, part_ref, half_ref):
        left = halves(panel_ref[...])
        for at in range(0, cols, TILE):
            part_ref[:, at : at + TILE] = dot3(left, halves(inv_ref[:, at : at + TILE]))
        half_ref[...] = part_ref[pl.ds(pl.multiple_of(sc[1] * half, half), half), :TILE]

    return call(
        body, "node_part", sc, [panel, inv], deps,
        [((upd, cols), F32), ((half, TILE), F32)], mflop=3000, mib=6,
    )


def node_lift(sc, part, mine, peer, rhs_low, rhs, index, deps):
    upd, cols = part.shape
    half = upd // 2
    width = rhs.shape[1]
    shapes = [
        ((upd, cols), BF16), ((upd, cols), BF16), ((cols, upd), BF16), ((cols, upd), BF16),
        ((upd, cols), F32), ((upd, width), F32),
    ]

    def body(sc, part_ref, mine_ref, peer_ref, low_ref, rhs_ref, index_ref, *rest):
        hi_ref, lo_ref, thi_ref, tlo_ref, whole_ref, base_ref = rest[-6:]

        @pl.when(sc[0] == 1)
        def _():
            first = sc[1] == 0
            m, p = mine_ref[...], peer_ref[...]
            whole_ref[...] = part_ref[...]
            whole_ref[:half, :TILE] += jnp.where(first, m, p)
            whole_ref[half:, :TILE] += jnp.where(first, p, m)
            split = halves(whole_ref[...])
            rhs_wide = jnp.concatenate([wide(low_ref[...]), wide(rhs_ref[...])], axis=0)
            base_ref[...] = times(split, rhs_wide)
            for at in range(0, cols, TILE):
                chosen = selection(index_ref[:, at : at + TILE], cols)
                value = exact(split, chosen)
                hi_ref[:, at : at + TILE], lo_ref[:, at : at + TILE] = halves(value)
                thi_ref[at : at + TILE, :], tlo_ref[at : at + TILE, :] = halves(value.T)

    ins = [part, mine, peer, rhs_low, rhs, index]
    return call(body, "node_lift", sc, ins, deps, shapes, vmem=40, mflop=4000, mib=12)


def node_top(sc, top, inv, rhs_low, rhs, index, deps):
    rows, cols = inv.shape
    width = rhs.shape[1]

    def body(sc, inv_ref, low_ref, rhs_ref, index_ref, out_ref):
        @pl.when(sc[2] == top)
        def _():
            split = halves(inv_ref[...])
            chosen = selection(index_ref[:, :TILE], cols)
            value = exact(split, chosen)
            own, low = wide(rhs_ref[...]), wide(low_ref[...])
            is_low = sc[0] == 0
            first = jnp.where(is_low, own.astype(F32), low.astype(F32)).astype(BF16)
            solved = times(split, jnp.concatenate([first, own], axis=0))
            left = halves(value.T)
            out_ref[:, :TILE] = dot3(left, halves(value))
            out_ref[:, TILE:] = dot3(left, halves(solved))

    return call(
        body, "node_top", sc, [inv, rhs_low, rhs, index], deps,
        [((TILE, TILE + width), F32)], mflop=2500, mib=5,
    )[0]


def node_select(sc, inv_low, inv, rhs_low, rhs, index, deps):
    rows, cols = inv.shape
    width = rhs.shape[1]

    def body(sc, inv_low_ref, inv_ref, low_ref, rhs_ref, index_ref, hi_ref, lo_ref, solved_ref):
        @pl.when(sc[0] == 1)
        def _():
            low_split, split = halves(inv_low_ref[...]), halves(inv_ref[...])
            low_wide = wide(low_ref[...])
            rhs_wide = jnp.concatenate([low_wide, wide(rhs_ref[...])], axis=0)
            solved_ref[:rows] = times(low_split, low_wide)
            solved_ref[rows:] = times(split, rhs_wide)
            for at in range(0, cols, TILE):
                chosen = selection(index_ref[:, at : at + TILE], cols)
                there = slice(at, at + TILE)
                hi_ref[:rows, there], lo_ref[:rows, there] = halves(exact(low_split, chosen[:rows]))
                hi_ref[rows:, there], lo_ref[rows:, there] = halves(exact(split, chosen))

    return call(
        body, "node_select", sc, [inv_low, inv, rhs_low, rhs, index], deps,
        [((cols, cols), BF16), ((cols, cols), BF16), ((cols, width), F32)],
        vmem=36, mflop=4000, mib=9,
    )


def climb(sc, level, base, hi, lo, pieces, kept, deps):
    upd, width = base.shape
    cols = hi.shape[1]
    n = len(pieces)

    def body(sc, base_ref, hi_ref, lo_ref, *refs):
        up_ref, kept_ref = refs[-2:]

        @pl.when((sc[0] == 1) & (sc[3] == level))
        def _():
            value = jnp.concatenate([r[...] for r in refs[:n]], axis=0)
            kept_ref[...] = value
            up_ref[...] = base_ref[...] - times((hi_ref[...], lo_ref[...]), wide(value))

    ins = [base, hi, lo, *pieces]
    aliases = None
    if kept is not None:
        aliases = {1 + len(ins): 1}
        ins = ins + [kept]
    return call(
        body, "climb", sc, ins, deps, [((upd, width), F32), ((cols, width), F32)],
        aliases=aliases, mflop=400, mib=3,
    )


def turn(sc, level, base, hi, lo, pieces, kept, top, inv_hi, inv_lo, solved, thi, tlo, deps):
    upd, width = base.shape
    cols = hi.shape[1]

    def body(sc, base_ref, hi_ref, lo_ref, l_ref, r_ref, kept_ref, top_a, top_b, ih_ref, il_ref,
             solved_ref, thi_ref, tlo_ref, up_ref, seen_ref, y_ref, from_up_ref, down_ref):
        is_top = sc[3] == level

        @pl.when(sc[0] == 1)
        def _():
            arrived = jnp.concatenate([l_ref[...], r_ref[...]], axis=0)
            u_wide = wide(jnp.where(is_top, arrived, kept_ref[...]))
            split = (ih_ref[...], il_ref[...])
            y = solved_ref[...] - times(split, u_wide)
            y_ref[...] = y
            from_up = under(tall(y.T), split).T
            from_up_ref[...] = from_up

            @pl.when(is_top)
            def _():
                up = base_ref[...] - times((hi_ref[...], lo_ref[...]), u_wide)
                up_ref[...] = up
                both = top_a[...] + top_b[...]
                seen = both[:, upd:] - times(halves(both[:, :upd]), wide(up))
                seen_ref[...] = seen
                down_ref[...] = from_up - times((thi_ref[...], tlo_ref[...]), wide(seen))

    return call(
        body, "turn", sc,
        [base, hi, lo, *pieces, kept, *top, inv_hi, inv_lo, solved, thi, tlo], deps,
        [((upd, width), F32), ((upd, width), F32), ((cols, width), F32), ((cols, width), F32),
         ((cols, width), F32)],
        vmem=36, mflop=1500, mib=12,
    )


def descend(sc, level, from_up, thi, tlo, pieces, kept, cuts, deps):
    cols, width = from_up.shape
    upd = kept.shape[0]
    n = len(pieces)

    def body(sc, from_ref, thi_ref, tlo_ref, *refs):
        outs = refs[n + 1 :]
        seen_ref = outs[0]

        @pl.when((sc[0] == 1) & (sc[3] == level))
        def _():
            value = refs[0][...]
            for ref in refs[1:n]:
                value += ref[...]
            seen_ref[...] = value
            z_wide = wide(value)
            at = 0
            for out in outs[1:]:
                size = out.shape[0]
                there = slice(at, at + size)
                out[...] = from_ref[there] - times((thi_ref[there], tlo_ref[there]), z_wide)
                at += size

    ins = [from_up, thi, tlo, *pieces, kept]
    return call(
        body, "descend", sc, ins, deps,
        [((upd, width), F32)] + [((size, width), F32) for size in cuts],
        aliases={len(ins): 0}, mflop=400, mib=3,
    )


def node_tail(sc, top, inv_low, inv, y, whole, seen, top_up, inv_hi, inv_lo, solved, deps):
    rows, cols = inv.shape
    width = y.shape[1]

    def body(sc, inv_low_ref, inv_ref, y_ref, whole_ref, seen_ref, up_ref, ih_ref, il_ref,
             solved_ref, low_ref, high_ref):
        def give(y, x):
            y_tall = tall(y.T)
            low_tall, high_tall = y_tall[:, :rows], y_tall[:, rows:]
            high_ref[...] = x[:, rows:] + under(high_tall, halves(inv_ref[:, rows:]))
            low_ref[...] = (
                x[:, :rows]
                + under(high_tall, halves(inv_ref[:, :rows]))
                + under(low_tall, halves(inv_low_ref[...]))
            )

        @pl.when((sc[0] == 1) & (sc[2] != top))
        def _():
            give(y_ref[...], -under(tall(seen_ref[...].T), halves(whole_ref[...])))

        @pl.when((sc[0] == 1) & (sc[2] == top))
        def _():
            split = (ih_ref[:, :TILE], il_ref[:, :TILE])
            give(solved_ref[...] - times(split, wide(up_ref[...])), jnp.zeros((width, cols), F32))

    return call(
        body, "node_tail", sc,
        [inv_low, inv, y, whole, seen, top_up, inv_hi, inv_lo, solved], deps,
        [((width, rows), F32), ((width, cols - rows), F32)], vmem=40, mflop=1500, mib=12,
    )


def finish(sc, leaf, node, squares, others, channels):
    width, rows = leaf.shape
    node_rows = node.shape[1]

    def body(sc, leaf_ref, node_ref, squares_ref, others_ref, leaf_out, node_out):
        scale = lax.rsqrt((squares_ref[...] + others_ref[...]) / channels + EPS)
        for at in range(0, rows, TILE):
            there = slice(at, at + TILE)
            leaf_out[there, :] = (leaf_ref[:, there] * scale[:, there]).T
        node_out[...] = (node_ref[...] * scale[:, rows:]).T

    return call(
        body, "finish", sc, [leaf, node, squares, others], [],
        [((rows, width), F32), ((node_rows, width), F32)], mflop=10, mib=3,
    )


def level_of(place, depth):
    level = 1
    while place % 2 == 1 and level <= depth:
        place //= 2
        level += 1
    return level


def after(value, *first):
    return lax.optimization_barrier((value,) + first)[0]


def on_device(leaf_rhs, node_rhs, leaf_inv, node_inv, leaf_panel, node_panel, leaf_rows, node_rows):
    count = lax.axis_size("subtree")
    depth = count.bit_length() - 1
    place = lax.axis_index("subtree").astype(jnp.int32)
    f = lax.axis_index("fshard").astype(jnp.int32)
    c = lax.axis_index("chan").astype(jnp.int32)
    level = jnp.ones((), jnp.int32)
    for bit in range(depth):
        level = level + ((place + 1) % 2 ** (bit + 1) == 0).astype(jnp.int32)
    sc = jnp.stack([f, c, place, level])
    low = f == 0
    is_even = place % 2 == 0
    width = leaf_rhs.shape[1]
    upd = leaf_rows.shape[1]
    half = upd // 2
    sep_half = node_rhs.shape[0]
    rows = leaf_rhs.shape[0]
    levels = [level_of(d, depth) for d in range(count)]
    everyone = range(count)
    evens, odds = range(0, count, 2), range(1, count, 2)
    top, sub = count - 1, count // 2 - 1

    def send(value, quads):
        pairs = [(2 * s + g, 2 * t + h) for s, g, t, h in quads]
        return lax.ppermute(value, ("subtree", "fshard"), pairs)

    def lift_over(value, places):
        return send(value, [(d, 0, d, 1) for d in places])

    def drop_over(value):
        return send(value, [(d, 1, d, 0) for d in everyone])

    def swap_chan(value, g):
        return lax.ppermute(value, ("chan", "fshard"), [(g, 2 + g), (2 + g, g)])

    left_kid = [(d - 2 ** (levels[d] - 2), d) for d in odds]
    right_kid = [(d + 2 ** (levels[d] - 2), d) for d in odds if levels[d] <= depth]

    piece_rows = rows // 2
    piece0 = lift_over(leaf_rhs[:piece_rows], everyone)
    part, part_half = node_part(sc, node_panel, node_inv, [])
    mine = lift_over(part_half, everyone)
    leaf_y, leaf_up = leaf_own(sc, leaf_inv, leaf_rhs, leaf_panel, [part])
    piece1 = lift_over(after(leaf_rhs[piece_rows:], piece0, leaf_up), everyone)
    up_low = lift_over(after(leaf_up, piece0), everyone)
    rhs_low = lift_over(after(node_rhs, piece0, leaf_up), everyone)
    y1 = leaf_other(sc, leaf_inv, piece0, leaf_y, 0, None, [leaf_up])[0]
    peer = swap_chan(after(mine, y1), 1)

    leaf_over = [(o, 1, (o + 1) % count, 1) for o in odds]
    leaf_under = [(o, 1, o - 1, 1) for o in odds]
    node_index, leaf_index = after((node_rows, leaf_rows), y1)
    leaf_l = send(leaf_index[:, half:], leaf_over)
    leaf_r = send(leaf_index[:, :half], leaf_under)
    from_left = send(node_index, [(s, g, t, g) for s, t in left_kid for g in (0, 1)])
    from_right = send(node_index, [(s, 1, t, 1) for s, t in right_kid])
    index = jnp.where(
        is_even,
        jnp.concatenate([leaf_index, leaf_l, leaf_r], axis=1),
        jnp.concatenate([from_left, jnp.where(place == top, -1, from_right)], axis=1),
    )

    leaf_y, leaf_up = leaf_other(sc, leaf_inv, piece1, y1, 1, leaf_panel, [])
    leaf_up = leaf_up + up_low
    inv_low = lift_over(after(node_inv[:, :sep_half], up_low, rhs_low, peer), everyone)

    from_l = send(leaf_up[half:], leaf_over)
    from_r = send(leaf_up[:half], leaf_under)
    hi, lo, thi, tlo, whole, base_up = node_lift(
        sc, part, mine, peer, rhs_low, node_rhs, index, [leaf_up]
    )
    node_up, kept = climb(sc, 1, base_up, hi, lo, [leaf_up, from_l, from_r], None, [])

    def rise(value, at):
        return [
            send(value, [(s, 1, t, 1) for s, t in kid if levels[t] == at])
            for kid in (left_kid, right_kid)
        ]

    got = rise(node_up, 2)
    pan0, back0 = back_other(sc, leaf_inv, leaf_y, leaf_panel, 0, [node_up])
    pan_mine0 = drop_over(pan0)
    top_part = node_top(sc, top, node_inv, rhs_low, node_rhs, index, [back0])
    tops = [send(top_part, [(top, g, sub, 1)]) for g in (0, 1)]
    node_up, kept = climb(sc, 2, base_up, hi, lo, got, kept, [top_part])
    got = rise(node_up, 3)
    pan1, back1 = back_other(sc, leaf_inv, leaf_y, leaf_panel, 2, [node_up])
    pan_mine1 = drop_over(pan1)
    back_mine0 = drop_over(after(back0, pan_mine1))
    back_mine1 = drop_over(after(back1, pan_mine1))
    node_up, kept = climb(sc, 3, base_up, hi, lo, got, kept, [back1])
    got = rise(node_up, 4)
    inv_hi, inv_lo, solved = node_select(
        sc, inv_low, node_inv, rhs_low, node_rhs, index, [node_up, *tops]
    )
    node_up, kept = climb(sc, 4, base_up, hi, lo, got, kept, [inv_hi])
    got = rise(node_up, 5)
    pan_peer0 = swap_chan(after(pan_mine0, node_up), 0)
    own0 = back_own(sc, leaf_inv, leaf_y, leaf_panel, [0], [node_up])
    top_up, seen, node_y, from_up, down = turn(
        sc, depth, base_up, hi, lo, got, kept, tops, inv_hi, inv_lo, solved, thi, tlo, [own0]
    )
    late_up = send(top_up, [(sub, 1, top, 1)])

    def fall(left, right, at):
        return [
            send(v, [(t, 1, s, 1) for s, t in kid if levels[t] == at])
            for v, kid in ((left, left_kid), (right, right_kid))
        ]

    got = fall(down[:upd], down[upd:], depth)
    own1 = back_own(sc, leaf_inv, leaf_y, leaf_panel, [1], [down])
    pan_peer1 = swap_chan(after(pan_mine1, pan_peer0, own1), 0)
    fill = [own1]
    for at in range(depth - 1, 1, -1):
        seen, left, right = descend(sc, at, from_up, thi, tlo, got, seen, (upd, upd), fill)
        got = fall(left, right, at)
        fill = []
        if at == depth - 1:
            own23 = back_own(sc, leaf_inv, leaf_y, leaf_panel, [2, 3], [left])
            fill = [own23]
    seen, mid, to_left, to_right = descend(
        sc, 1, from_up, thi, tlo, got, seen, (upd, half, half),
        [back_mine0, back_mine1, pan_peer0, pan_peer1],
    )
    seen_odd = [
        send(v, [(e, 1, (e + by) % count, g) for e in evens])
        for v, by in ((to_right, 1), (to_left, -1))
        for g in (1, 0)
    ]
    seen_own = send(mid, [(e, 1, e, 0) for e in evens])
    node_low, node_high = node_tail(
        sc, top, inv_low, node_inv, node_y, whole, seen, late_up, inv_hi, inv_lo, solved, [to_right]
    )
    leaf_x, node_x, squares = leaf_tail(
        sc, [own0, own1, own23], [pan_mine0, pan_mine1], [pan_peer0, pan_peer1],
        [back_mine0, back_mine1], [seen_own, mid, *seen_odd], [drop_over(after(node_low, seen_odd[0])), node_high], [],
    )
    others = lax.ppermute(squares, "chan", [(0, 1), (1, 0)])
    channels = float(width * lax.axis_size("chan"))
    return tuple(finish(sc, leaf_x, node_x, squares, others, channels))


def solution(mesh):
    in_specs = (
        P(("subtree", "fshard"), "chan"),
        P(("subtree", "fshard"), "chan"),
        P(("subtree", "fshard"), None),
        P(("subtree", "fshard"), None),
        P("subtree", "fshard"),
        P("subtree", "fshard"),
        P("subtree", None),
        P("subtree", None),
    )
    out_specs = (P(("subtree", "fshard"), "chan"), P(("subtree", "fshard"), "chan"))
    return jax.shard_map(
        on_device, mesh=mesh, in_specs=in_specs, out_specs=out_specs, check_vma=False
    )
```

```python
import jax
import jax.numpy as jnp
from jax import lax
from jax.experimental import pallas as pl
from jax.experimental.pallas import tpu as pltpu
from jax.sharding import PartitionSpec as P

EPS = 1e-06
F32 = jnp.float32
BF16 = jnp.bfloat16
TILE = 512
MIB = 1024 * 1024


def halves(value):
    high = value.astype(BF16)
    return high, (value - high.astype(F32)).astype(BF16)


def mm(left, right):
    return jnp.dot(left, right, preferred_element_type=F32)


def wide(value):
    return jnp.concatenate(halves(value), axis=1)


def tall(value):
    return jnp.concatenate(halves(value), axis=0)


def times(split, right_wide):
    total = mm(split[0], right_wide) + mm(split[1], right_wide)
    width = total.shape[1] // 2
    return total[:, :width] + total[:, width:]


def under(left_tall, split):
    total = mm(left_tall, split[0]) + mm(left_tall, split[1])
    height = total.shape[0] // 2
    return total[:height] + total[height:]


def dot3(left, right):
    return mm(left[0], right[0]) + (mm(left[0], right[1]) + mm(left[1], right[0]))


def exact(split, chosen):
    return mm(split[0], chosen) + mm(split[1], chosen)


def selection(index_row, height):
    rows = lax.broadcasted_iota(jnp.int32, (height, index_row.shape[1]), 0)
    return (rows == index_row).astype(F32).astype(BF16)


ANY = pl.BlockSpec(memory_space=pl.ANY)
SMEM = pl.BlockSpec(memory_space=pltpu.SMEM)
VMEM = pl.BlockSpec(memory_space=pltpu.VMEM)


def cost(mflop, mib):
    return pl.CostEstimate(flops=mflop * 10**6, bytes_accessed=mib * 1024, transcendentals=0)


def call(body, name, scalars, ins, deps, outs, aliases=None, vmem=24, mflop=500, mib=4):
    n_in, n_dep = len(ins), len(deps)

    def kernel(*refs):
        body(refs[0], *refs[1 : 1 + n_in], *refs[1 + n_in + n_dep :])

    return pl.pallas_call(
        kernel,
        in_specs=[SMEM] + [VMEM] * n_in + [ANY] * n_dep,
        out_specs=[VMEM] * len(outs),
        out_shape=[jax.ShapeDtypeStruct(s, t) for s, t in outs],
        input_output_aliases=aliases or {},
        compiler_params=pltpu.CompilerParams(vmem_limit_bytes=vmem * MIB),
        cost_estimate=cost(mflop, mib),
        name=name,
    )(scalars, *ins, *deps)


def tiled(body, name, scalars, grid, ins, deps, outs, scratch=(), aliases=None, vmem=28, mflop=4000, mib=12):
    n_in, n_dep = len(ins), len(deps)
    n_s = len(scalars)

    def kernel(*refs):
        body(*refs[: n_s + n_in], *refs[n_s + n_in + n_dep :])

    return pl.pallas_call(
        kernel,
        grid_spec=pltpu.PrefetchScalarGridSpec(
            num_scalar_prefetch=n_s,
            grid=grid,
            in_specs=[pl.BlockSpec(b, m) for _, b, m in ins] + [ANY] * n_dep,
            out_specs=[pl.BlockSpec(b, m) for _, b, m in outs],
            scratch_shapes=list(scratch),
        ),
        out_shape=[jax.ShapeDtypeStruct(s, F32) for s, _, _ in outs],
        input_output_aliases=aliases or {},
        compiler_params=pltpu.CompilerParams(vmem_limit_bytes=vmem * MIB),
        cost_estimate=cost(mflop, mib),
        name=name,
    )(*scalars, *[v for v, _, _ in ins], *deps)


def rows_of(ref, block, size=TILE):
    return ref[pl.ds(pl.multiple_of(block * size, size), size), :]


def leaf_own(sc, inv, rhs, panel, deps):
    rows, width = rhs.shape
    upd = panel.shape[0]
    tile = 2 * TILE
    n = rows // tile
    steps = [(i, j) for i in range(n) for j in range(i + 1)]
    at_i = jnp.array([i for i, _ in steps], jnp.int32)
    at_j = jnp.array([j for _, j in steps], jnp.int32)

    def body(sc, ti, tj, inv_ref, rhs_ref, panel_ref, y_ref, up_ref, rhs_wide):
        s = pl.program_id(0)
        i, j = ti[s], tj[s]

        @pl.when(s == 0)
        def _():
            rhs_wide[...] = wide(rhs_ref[...])
            up_ref[...] = jnp.zeros_like(up_ref)

        value = times(halves(inv_ref[...]), rows_of(rhs_wide, j, tile))

        @pl.when(j == 0)
        def _():
            y_ref[...] = value

        @pl.when(j > 0)
        def _():
            y_ref[...] += value

        @pl.when((j == i) & (sc[0] == 0))
        def _():
            up_ref[...] += times(halves(panel_ref[...]), wide(y_ref[...]))

    return tiled(
        body, "leaf_own", (sc, at_i, at_j), (len(steps),),
        [
            (inv, (tile, tile), lambda s, sc, ti, tj: (ti[s], sc[0] * n + tj[s])),
            (rhs, (rows, width), lambda s, *_: (0, 0)),
            (panel, (upd, tile), lambda s, sc, ti, tj: (0, ti[s])),
        ],
        deps,
        [
            ((rows, width), (tile, width), lambda s, sc, ti, tj: (ti[s], 0)),
            ((upd, width), (upd, width), lambda s, *_: (0, 0)),
        ],
        vmem=40,
        scratch=[pltpu.VMEM((rows, 2 * width), BF16)],
    )


def leaf_other(sc, inv, piece, y, step, panel, deps):
    rows, width = y.shape
    depth = piece.shape[0]
    tile = 2 * TILE
    whole = lambda i, sc: (0, 0)
    ins = [
        (inv, (tile, depth), lambda i, sc: (i * sc[0], step * sc[0])),
        (piece, (depth, width), whole),
        (y, (tile, width), lambda i, sc: (i, 0)),
    ]
    outs = [((rows, width), (tile, width), lambda i, sc: (i, 0))]
    if panel is not None:
        upd = panel.shape[0]
        ins.append((panel, (upd, tile), lambda i, sc: (0, i * sc[0])))
        outs.append(((upd, width), (upd, width), whole))

    def body(sc, inv_ref, piece_ref, y_in, *rest):
        *rest, piece_wide = rest
        i = pl.program_id(0)

        @pl.when(i == 0)
        def _():
            piece_wide[...] = wide(piece_ref[...])

        if panel is None:
            (y_ref,) = rest
        else:
            panel_ref, y_ref, up_ref = rest

        @pl.when(sc[0] == 0)
        def _():
            y_ref[...] = y_in[...]

        @pl.when(sc[0] == 1)
        def _():
            value = y_in[...] + times(halves(inv_ref[...]), piece_wide[...])
            y_ref[...] = value
            if panel is not None:
                lift = times(halves(panel_ref[...]), wide(value))

                @pl.when(i == 0)
                def _():
                    up_ref[...] = lift

                @pl.when(i > 0)
                def _():
                    up_ref[...] += lift

    return tiled(
        body, "leaf_other", (sc,), (rows // tile,), ins, deps, outs,
        scratch=[pltpu.VMEM((depth, 2 * width), BF16)], mflop=6000, mib=12, vmem=40,
    )


def back_other(sc, inv, y, panel, first, deps):
    rows, width = y.shape
    upd = panel.shape[0]
    half = upd // 2

    def body(sc, panel_ref, y_ref, inv_ref, lift_ref, back_ref, hi_ref, lo_ref):
        @pl.when(sc[0] == 1)
        def _():
            @pl.when(pl.program_id(0) == 0)
            def _():
                hi_ref[:half, :], lo_ref[:half, :] = halves(panel_ref[...])
                hi_ref[half:, :], lo_ref[half:, :] = halves(y_ref[...].T)

            value = dot3((hi_ref[...], lo_ref[...]), halves(inv_ref[...]))
            lift_ref[...] = value[:half]
            back_ref[...] = value[half:]

    return tiled(
        body, "back_other", (sc,), (2,),
        [
            (panel, (half, rows), lambda j, sc: (sc[1] * sc[0], 0)),
            (y, (rows, width), lambda j, sc: (0, 0)),
            (inv, (rows, TILE), lambda j, sc: (0, (first + j) * sc[0])),
        ],
        deps,
        [
            ((half, 2 * TILE), (half, TILE), lambda j, sc: (0, j)),
            ((width, 2 * TILE), (width, TILE), lambda j, sc: (0, j)),
        ],
        scratch=[pltpu.VMEM((half + width, rows), BF16)] * 2,
        mflop=4000, mib=12, vmem=32,
    )


def back_own(sc, inv, y, panel, columns, deps):
    rows, width = y.shape
    upd = panel.shape[0]
    n = rows // TILE
    steps = [(j, i) for j in columns for i in range(j, n)]
    at_j = jnp.array([j for j, _ in steps], jnp.int32)
    at_i = jnp.array([i for _, i in steps], jnp.int32)
    base = columns[0]

    def body(sc, tj, ti, y_ref, panel_ref, inv_ref, out_ref):
        s = pl.program_id(0)
        block = halves(inv_ref[...])
        back = under(tall(y_ref[...].T), block)
        lift = dot3(halves(panel_ref[...]), block)

        @pl.when(ti[s] == tj[s])
        def _():
            out_ref[:width, :] = back
            out_ref[width:, :] = lift

        @pl.when(ti[s] > tj[s])
        def _():
            out_ref[:width, :] += back
            out_ref[width:, :] += lift

    return tiled(
        body, "back_own", (sc, at_j, at_i), (len(steps),),
        [
            (y, (TILE, width), lambda s, sc, tj, ti: (ti[s], 0)),
            (panel, (upd, TILE), lambda s, sc, tj, ti: (0, ti[s])),
            (inv, (TILE, TILE), lambda s, sc, tj, ti: (ti[s], sc[0] * n + tj[s])),
        ],
        deps,
        [
            (
                (width + upd, TILE * len(columns)),
                (width + upd, TILE),
                lambda s, sc, tj, ti: (0, tj[s] - base),
            )
        ],
        mflop=1000 * len(steps), mib=2 * len(steps), vmem=18,
    )[0]


def leaf_tail(sc, own, mine, peer, back, seen, node, deps):
    half, width = seen[2].shape
    sep_half = node[0].shape[1]
    n = len(own)

    def body(sc, *refs):
        own_refs, mine_refs, peer_refs = refs[:n], refs[n : n + 2], refs[n + 2 : n + 4]
        back_refs, seen_refs, node_refs = refs[n + 4 : n + 6], refs[n + 6 : n + 12], refs[n + 12 : n + 14]
        x_ref, node_ref, squares_ref = refs[n + 14 :]
        is_low = sc[0] == 0
        whole = jnp.where(is_low, seen_refs[0][...], seen_refs[1][...])
        parts = jnp.concatenate(
            [seen_refs[2][...] + seen_refs[3][...], seen_refs[4][...] + seen_refs[5][...]], axis=0
        )
        seen_tall = tall(jnp.where(sc[2] % 2 == 0, whole, parts).T)
        first = sc[1] == 0
        col = 0
        for own_ref in own_refs:
            for at in range(0, own_ref.shape[1], TILE):
                which, inner = col // 2, (col % 2) * TILE
                cols, take = slice(at, at + TILE), slice(inner, inner + TILE)
                m, p = mine_refs[which][:, take], peer_refs[which][:, take]
                lift = own_ref[width:, cols] + jnp.concatenate(
                    [jnp.where(first, m, p), jnp.where(first, p, m)], axis=0
                )
                base = own_ref[:width, cols] + back_refs[which][:, take]
                x = base - under(seen_tall, halves(lift))
                out = slice(col * TILE, (col + 1) * TILE)
                x_ref[:, out] = x
                squares_ref[:, out] = jnp.sum(x * x, axis=0, keepdims=True)
                col += 1
        node_x = jnp.where(is_low, node_refs[0][...], node_refs[1][...])
        node_ref[...] = node_x
        squares_ref[:, col * TILE :] = jnp.sum(node_x * node_x, axis=0, keepdims=True)

    total = sum(v.shape[1] for v in own)
    return call(
        body, "leaf_tail", sc, [*own, *mine, *peer, *back, *seen, *node], deps,
        [((width, total), F32), ((width, sep_half), F32), ((1, total + sep_half), F32)],
        vmem=40, mflop=1000, mib=14,
    )


def node_part(sc, panel, inv, deps):
    upd = panel.shape[0]
    half = upd // 2
    cols = inv.shape[1]

    def body(sc, panel_ref, inv_ref, part_ref, half_ref):
        left = halves(panel_ref[...])
        for at in range(0, cols, TILE):
            part_ref[:, at : at + TILE] = dot3(left, halves(inv_ref[:, at : at + TILE]))
        half_ref[...] = part_ref[pl.ds(pl.multiple_of(sc[1] * half, half), half), :TILE]

    return call(
        body, "node_part", sc, [panel, inv], deps,
        [((upd, cols), F32), ((half, TILE), F32)], mflop=3000, mib=6,
    )


def node_lift(sc, part, mine, peer, rhs_low, rhs, index, deps):
    upd, cols = part.shape
    half = upd // 2
    width = rhs.shape[1]
    shapes = [
        ((upd, cols), BF16), ((upd, cols), BF16), ((cols, upd), BF16), ((cols, upd), BF16),
        ((upd, cols), F32), ((upd, width), F32),
    ]

    def body(sc, part_ref, mine_ref, peer_ref, low_ref, rhs_ref, index_ref, *rest):
        hi_ref, lo_ref, thi_ref, tlo_ref, whole_ref, base_ref = rest[-6:]

        @pl.when(sc[0] == 1)
        def _():
            first = sc[1] == 0
            m, p = mine_ref[...], peer_ref[...]
            whole_ref[...] = part_ref[...]
            whole_ref[:half, :TILE] += jnp.where(first, m, p)
            whole_ref[half:, :TILE] += jnp.where(first, p, m)
            split = halves(whole_ref[...])
            rhs_wide = jnp.concatenate([wide(low_ref[...]), wide(rhs_ref[...])], axis=0)
            base_ref[...] = times(split, rhs_wide)
            for at in range(0, cols, TILE):
                chosen = selection(index_ref[:, at : at + TILE], cols)
                value = exact(split, chosen)
                hi_ref[:, at : at + TILE], lo_ref[:, at : at + TILE] = halves(value)
                thi_ref[at : at + TILE, :], tlo_ref[at : at + TILE, :] = halves(value.T)

    ins = [part, mine, peer, rhs_low, rhs, index]
    return call(body, "node_lift", sc, ins, deps, shapes, vmem=40, mflop=4000, mib=12)


def node_top(sc, top, inv, rhs_low, rhs, index, deps):
    rows, cols = inv.shape
    width = rhs.shape[1]

    def body(sc, inv_ref, low_ref, rhs_ref, index_ref, out_ref):
        @pl.when(sc[2] == top)
        def _():
            split = halves(inv_ref[...])
            chosen = selection(index_ref[:, :TILE], cols)
            value = exact(split, chosen)
            own, low = wide(rhs_ref[...]), wide(low_ref[...])
            is_low = sc[0] == 0
            first = jnp.where(is_low, own.astype(F32), low.astype(F32)).astype(BF16)
            solved = times(split, jnp.concatenate([first, own], axis=0))
            left = halves(value.T)
            out_ref[:, :TILE] = dot3(left, halves(value))
            out_ref[:, TILE:] = dot3(left, halves(solved))

    return call(
        body, "node_top", sc, [inv, rhs_low, rhs, index], deps,
        [((TILE, TILE + width), F32)], mflop=2500, mib=5,
    )[0]


def node_select(sc, inv_low, inv, rhs_low, rhs, index, deps):
    rows, cols = inv.shape
    width = rhs.shape[1]

    def body(sc, inv_low_ref, inv_ref, low_ref, rhs_ref, index_ref, hi_ref, lo_ref, solved_ref):
        @pl.when(sc[0] == 1)
        def _():
            low_split, split = halves(inv_low_ref[...]), halves(inv_ref[...])
            low_wide = wide(low_ref[...])
            rhs_wide = jnp.concatenate([low_wide, wide(rhs_ref[...])], axis=0)
            solved_ref[:rows] = times(low_split, low_wide)
            solved_ref[rows:] = times(split, rhs_wide)
            for at in range(0, cols, TILE):
                chosen = selection(index_ref[:, at : at + TILE], cols)
                there = slice(at, at + TILE)
                hi_ref[:rows, there], lo_ref[:rows, there] = halves(exact(low_split, chosen[:rows]))
                hi_ref[rows:, there], lo_ref[rows:, there] = halves(exact(split, chosen))

    return call(
        body, "node_select", sc, [inv_low, inv, rhs_low, rhs, index], deps,
        [((cols, cols), BF16), ((cols, cols), BF16), ((cols, width), F32)],
        vmem=36, mflop=4000, mib=9,
    )


def climb(sc, level, base, hi, lo, pieces, kept, deps):
    upd, width = base.shape
    cols = hi.shape[1]
    n = len(pieces)

    def body(sc, base_ref, hi_ref, lo_ref, *refs):
        up_ref, kept_ref = refs[-2:]

        @pl.when((sc[0] == 1) & (sc[3] == level))
        def _():
            value = jnp.concatenate([r[...] for r in refs[:n]], axis=0)
            kept_ref[...] = value
            up_ref[...] = base_ref[...] - times((hi_ref[...], lo_ref[...]), wide(value))

    ins = [base, hi, lo, *pieces]
    aliases = None
    if kept is not None:
        aliases = {1 + len(ins): 1}
        ins = ins + [kept]
    return call(
        body, "climb", sc, ins, deps, [((upd, width), F32), ((cols, width), F32)],
        aliases=aliases, mflop=400, mib=3,
    )


def turn(sc, level, base, hi, lo, pieces, kept, top, inv_hi, inv_lo, solved, thi, tlo, deps):
    upd, width = base.shape
    cols = hi.shape[1]

    def body(sc, base_ref, hi_ref, lo_ref, l_ref, r_ref, kept_ref, top_a, top_b, ih_ref, il_ref,
             solved_ref, thi_ref, tlo_ref, up_ref, seen_ref, y_ref, from_up_ref, down_ref):
        is_top = sc[3] == level

        @pl.when(sc[0] == 1)
        def _():
            arrived = jnp.concatenate([l_ref[...], r_ref[...]], axis=0)
            u_wide = wide(jnp.where(is_top, arrived, kept_ref[...]))
            split = (ih_ref[...], il_ref[...])
            y = solved_ref[...] - times(split, u_wide)
            y_ref[...] = y
            from_up = under(tall(y.T), split).T
            from_up_ref[...] = from_up

            @pl.when(is_top)
            def _():
                up = base_ref[...] - times((hi_ref[...], lo_ref[...]), u_wide)
                up_ref[...] = up
                both = top_a[...] + top_b[...]
                seen = both[:, upd:] - times(halves(both[:, :upd]), wide(up))
                seen_ref[...] = seen
                down_ref[...] = from_up - times((thi_ref[...], tlo_ref[...]), wide(seen))

    return call(
        body, "turn", sc,
        [base, hi, lo, *pieces, kept, *top, inv_hi, inv_lo, solved, thi, tlo], deps,
        [((upd, width), F32), ((upd, width), F32), ((cols, width), F32), ((cols, width), F32),
         ((cols, width), F32)],
        vmem=36, mflop=1500, mib=12,
    )


def descend(sc, level, from_up, thi, tlo, pieces, kept, cuts, deps):
    cols, width = from_up.shape
    upd = kept.shape[0]
    n = len(pieces)

    def body(sc, from_ref, thi_ref, tlo_ref, *refs):
        outs = refs[n + 1 :]
        seen_ref = outs[0]

        @pl.when((sc[0] == 1) & (sc[3] == level))
        def _():
            value = refs[0][...]
            for ref in refs[1:n]:
                value += ref[...]
            seen_ref[...] = value
            z_wide = wide(value)
            at = 0
            for out in outs[1:]:
                size = out.shape[0]
                there = slice(at, at + size)
                out[...] = from_ref[there] - times((thi_ref[there], tlo_ref[there]), z_wide)
                at += size

    ins = [from_up, thi, tlo, *pieces, kept]
    return call(
        body, "descend", sc, ins, deps,
        [((upd, width), F32)] + [((size, width), F32) for size in cuts],
        aliases={len(ins): 0}, mflop=400, mib=3,
    )


def node_tail(sc, top, inv_low, inv, y, whole, seen, top_up, inv_hi, inv_lo, solved, deps):
    rows, cols = inv.shape
    width = y.shape[1]

    def body(sc, inv_low_ref, inv_ref, y_ref, whole_ref, seen_ref, up_ref, ih_ref, il_ref,
             solved_ref, low_ref, high_ref):
        def give(y, x):
            y_tall = tall(y.T)
            low_tall, high_tall = y_tall[:, :rows], y_tall[:, rows:]
            high_ref[...] = x[:, rows:] + under(high_tall, halves(inv_ref[:, rows:]))
            low_ref[...] = (
                x[:, :rows]
                + under(high_tall, halves(inv_ref[:, :rows]))
                + under(low_tall, halves(inv_low_ref[...]))
            )

        @pl.when((sc[0] == 1) & (sc[2] != top))
        def _():
            give(y_ref[...], -under(tall(seen_ref[...].T), halves(whole_ref[...])))

        @pl.when((sc[0] == 1) & (sc[2] == top))
        def _():
            split = (ih_ref[:, :TILE], il_ref[:, :TILE])
            give(solved_ref[...] - times(split, wide(up_ref[...])), jnp.zeros((width, cols), F32))

    return call(
        body, "node_tail", sc,
        [inv_low, inv, y, whole, seen, top_up, inv_hi, inv_lo, solved], deps,
        [((width, rows), F32), ((width, cols - rows), F32)], vmem=40, mflop=1500, mib=12,
    )


def finish(sc, leaf, node, squares, others, channels):
    width, rows = leaf.shape
    node_rows = node.shape[1]

    def body(sc, leaf_ref, node_ref, squares_ref, others_ref, leaf_out, node_out):
        scale = lax.rsqrt((squares_ref[...] + others_ref[...]) / channels + EPS)
        for at in range(0, rows, TILE):
            there = slice(at, at + TILE)
            leaf_out[there, :] = (leaf_ref[:, there] * scale[:, there]).T
        node_out[...] = (node_ref[...] * scale[:, rows:]).T

    return call(
        body, "finish", sc, [leaf, node, squares, others], [],
        [((rows, width), F32), ((node_rows, width), F32)], mflop=10, mib=3,
    )


def level_of(place, depth):
    level = 1
    while place % 2 == 1 and level <= depth:
        place //= 2
        level += 1
    return level


def after(value, *first):
    return lax.optimization_barrier((value,) + first)[0]


def on_device(leaf_rhs, node_rhs, leaf_inv, node_inv, leaf_panel, node_panel, leaf_rows, node_rows):
    count = lax.axis_size("subtree")
    depth = count.bit_length() - 1
    place = lax.axis_index("subtree").astype(jnp.int32)
    f = lax.axis_index("fshard").astype(jnp.int32)
    c = lax.axis_index("chan").astype(jnp.int32)
    level = jnp.ones((), jnp.int32)
    for bit in range(depth):
        level = level + ((place + 1) % 2 ** (bit + 1) == 0).astype(jnp.int32)
    sc = jnp.stack([f, c, place, level])
    low = f == 0
    is_even = place % 2 == 0
    width = leaf_rhs.shape[1]
    upd = leaf_rows.shape[1]
    half = upd // 2
    sep_half = node_rhs.shape[0]
    rows = leaf_rhs.shape[0]
    levels = [level_of(d, depth) for d in range(count)]
    everyone = range(count)
    evens, odds = range(0, count, 2), range(1, count, 2)
    top, sub = count - 1, count // 2 - 1

    def send(value, quads):
        pairs = [(2 * s + g, 2 * t + h) for s, g, t, h in quads]
        return lax.ppermute(value, ("subtree", "fshard"), pairs)

    def lift_over(value, places):
        return send(value, [(d, 0, d, 1) for d in places])

    def drop_over(value):
        return send(value, [(d, 1, d, 0) for d in everyone])

    def swap_chan(value, g):
        return lax.ppermute(value, ("chan", "fshard"), [(g, 2 + g), (2 + g, g)])

    left_kid = [(d - 2 ** (levels[d] - 2), d) for d in odds]
    right_kid = [(d + 2 ** (levels[d] - 2), d) for d in odds if levels[d] <= depth]

    piece_rows = rows // 2
    piece0 = lift_over(leaf_rhs[:piece_rows], everyone)
    part, part_half = node_part(sc, node_panel, node_inv, [])
    mine = lift_over(part_half, everyone)
    leaf_y, leaf_up = leaf_own(sc, leaf_inv, leaf_rhs, leaf_panel, [part])
    piece1 = lift_over(after(leaf_rhs[piece_rows:], piece0, leaf_up), everyone)
    up_low = lift_over(after(leaf_up, piece0), everyone)
    rhs_low = lift_over(after(node_rhs, piece0, leaf_up), everyone)
    y1 = leaf_other(sc, leaf_inv, piece0, leaf_y, 0, None, [leaf_up])[0]
    peer = swap_chan(after(mine, y1), 1)

    leaf_over = [(o, 1, (o + 1) % count, 1) for o in odds]
    leaf_under = [(o, 1, o - 1, 1) for o in odds]
    node_index, leaf_index = after((node_rows, leaf_rows), part)
    leaf_l = send(leaf_index[:, half:], leaf_over)
    leaf_r = send(leaf_index[:, :half], leaf_under)
    from_left = send(node_index, [(s, g, t, g) for s, t in left_kid for g in (0, 1)])
    from_right = send(node_index, [(s, 1, t, 1) for s, t in right_kid])
    index = jnp.where(
        is_even,
        jnp.concatenate([leaf_index, leaf_l, leaf_r], axis=1),
        jnp.concatenate([from_left, jnp.where(place == top, -1, from_right)], axis=1),
    )

    leaf_y, leaf_up = leaf_other(sc, leaf_inv, piece1, y1, 1, leaf_panel, [])
    leaf_up = leaf_up + up_low
    inv_low = lift_over(after(node_inv[:, :sep_half], up_low, rhs_low), everyone)

    from_l = send(leaf_up[half:], leaf_over)
    from_r = send(leaf_up[:half], leaf_under)
    hi, lo, thi, tlo, whole, base_up = node_lift(
        sc, part, mine, peer, rhs_low, node_rhs, index, [leaf_up]
    )
    node_up, kept = climb(sc, 1, base_up, hi, lo, [leaf_up, from_l, from_r], None, [])

    def rise(value, at):
        return [
            send(value, [(s, 1, t, 1) for s, t in kid if levels[t] == at])
            for kid in (left_kid, right_kid)
        ]

    got = rise(node_up, 2)
    pan0, back0 = back_other(sc, leaf_inv, leaf_y, leaf_panel, 0, [node_up])
    pan_mine0 = drop_over(pan0)
    top_part = node_top(sc, top, node_inv, rhs_low, node_rhs, index, [back0])
    tops = [send(top_part, [(top, g, sub, 1)]) for g in (0, 1)]
    node_up, kept = climb(sc, 2, base_up, hi, lo, got, kept, [top_part])
    got = rise(node_up, 3)
    pan1, back1 = back_other(sc, leaf_inv, leaf_y, leaf_panel, 2, [node_up])
    pan_mine1 = drop_over(pan1)
    back_mine0 = drop_over(after(back0, pan_mine1))
    back_mine1 = drop_over(after(back1, pan_mine1))
    node_up, kept = climb(sc, 3, base_up, hi, lo, got, kept, [back1])
    got = rise(node_up, 4)
    inv_hi, inv_lo, solved = node_select(
        sc, inv_low, node_inv, rhs_low, node_rhs, index, [node_up, *tops]
    )
    node_up, kept = climb(sc, 4, base_up, hi, lo, got, kept, [inv_hi])
    got = rise(node_up, 5)
    pan_peer0 = swap_chan(after(pan_mine0, node_up), 0)
    own0 = back_own(sc, leaf_inv, leaf_y, leaf_panel, [0], [node_up])
    top_up, seen, node_y, from_up, down = turn(
        sc, depth, base_up, hi, lo, got, kept, tops, inv_hi, inv_lo, solved, thi, tlo, [own0]
    )
    late_up = send(top_up, [(sub, 1, top, 1)])

    def fall(left, right, at):
        return [
            send(v, [(t, 1, s, 1) for s, t in kid if levels[t] == at])
            for v, kid in ((left, left_kid), (right, right_kid))
        ]

    got = fall(down[:upd], down[upd:], depth)
    own1 = back_own(sc, leaf_inv, leaf_y, leaf_panel, [1], [down])
    pan_peer1 = swap_chan(after(pan_mine1, pan_peer0, own1), 0)
    fill = [own1]
    for at in range(depth - 1, 1, -1):
        seen, left, right = descend(sc, at, from_up, thi, tlo, got, seen, (upd, upd), fill)
        got = fall(left, right, at)
        fill = []
        if at == depth - 1:
            own23 = back_own(sc, leaf_inv, leaf_y, leaf_panel, [2, 3], [left])
            fill = [own23]
    seen, mid, to_left, to_right = descend(
        sc, 1, from_up, thi, tlo, got, seen, (upd, half, half),
        [back_mine0, back_mine1, pan_peer0, pan_peer1],
    )
    seen_odd = [
        send(v, [(e, 1, (e + by) % count, g) for e in evens])
        for v, by in ((to_right, 1), (to_left, -1))
        for g in (1, 0)
    ]
    seen_own = send(mid, [(e, 1, e, 0) for e in evens])
    node_low, node_high = node_tail(
        sc, top, inv_low, node_inv, node_y, whole, seen, late_up, inv_hi, inv_lo, solved, [to_right]
    )
    leaf_x, node_x, squares = leaf_tail(
        sc, [own0, own1, own23], [pan_mine0, pan_mine1], [pan_peer0, pan_peer1],
        [back_mine0, back_mine1], [seen_own, mid, *seen_odd], [drop_over(after(node_low, seen_odd[0])), node_high], [],
    )
    others = lax.ppermute(squares, "chan", [(0, 1), (1, 0)])
    channels = float(width * lax.axis_size("chan"))
    return tuple(finish(sc, leaf_x, node_x, squares, others, channels))


def solution(mesh):
    in_specs = (
        P(("subtree", "fshard"), "chan"),
        P(("subtree", "fshard"), "chan"),
        P(("subtree", "fshard"), None),
        P(("subtree", "fshard"), None),
        P("subtree", "fshard"),
        P("subtree", "fshard"),
        P("subtree", None),
        P("subtree", None),
    )
    out_specs = (P(("subtree", "fshard"), "chan"), P(("subtree", "fshard"), "chan"))
    return jax.shard_map(
        on_device, mesh=mesh, in_specs=in_specs, out_specs=out_specs, check_vma=False
    )
```
